32 devices in a mesh: tm: 4 (over z), pairs: 8 (over y, x, core).
Axes of the slice: x: 2, y: 2, z: 4, core: 2. Of those that a mesh axis runs over, the one named last changes fastest.
Arguments:
- record: bfloat16 [32, 3, 4, 4096], P('pairs', None, 'tm')
- requested: int32 [8, 8, 2], replicated, may hold values from 0 to 3, as said below
- partners: int32 [8, 12, 48], P('pairs'), may hold values from 0 to 15
- codes: int32 [8, 12, 48], P('pairs'), may hold values from 0 to 2
- counts: int32 [8, 12], P('pairs'), may hold values from 1 to 48, as said below
Outputs:
- stacks: float32 [8, 576, 1024], P('pairs', 'tm')
The draws below stay inside these ranges and needn't reach their ends.
Inputs may be any that keep to these rules, and one draw needn't show every extreme that they name: requested[e, d] holds 2 different local station indices of device d, meaning stations d * 4 + requested[e, d, i]. `partners`: slot k stands for the station requested[e, k // 2, k % 2]. Slots at and after counts[e, j] are unused; on some device every owned trace has 48 live slots.
All inputs are finite; a program needn't handle non-finite values.
Results may differ from the reference program's by a relative error of at most 0.0037.
Values may be sent and summed in bfloat16 or wider, within the bound.
A program may use at most 64 MiB of HBM per device.

```python
import math
import jax
import jax.numpy as jnp
from jax import lax

S_DEV = 4
PER = 48
CAP = 2
WIN = 4096
LAGS = 1024
OWNERS = 8
STATIONS = 32
WINDOWS = 4


def draw_record(key, part):
    noise_key, scale_key = jax.random.split(key, 2)
    shape_all = (STATIONS, 3, WINDOWS, WIN)
    shape_amp = (STATIONS, 3, WINDOWS, 1)
    noise_part = jnp.clip(jax.random.normal(noise_key, shape_all, jnp.float32), -6.0, 6.0)
    scales = jnp.exp(jax.random.uniform(scale_key, shape_amp, jnp.float32, 0.0, math.log(10.0)))
    return (noise_part * scales).astype(jnp.bfloat16)


def draw_requested(key, part):
    scores = jax.random.randint(key, (OWNERS, OWNERS, S_DEV), 0, 1 << 20)
    scores = scores * S_DEV + jnp.arange(S_DEV, dtype=jnp.int32)[None, None, :]
    order = jnp.argsort(scores, axis=-1, stable=True)
    return order[..., :CAP].astype(jnp.int32)


def draw_counts(key, part):
    base_key, cut_key, full_key = jax.random.split(key, 3)
    base_load = jax.random.randint(base_key, (OWNERS, 1), max(PER // 4, 1), PER + 1)
    cut_rows = jax.random.randint(cut_key, (OWNERS, 3 * S_DEV), 0, PER + 1) % (base_load // 4 + 1)
    full_owner = jax.random.randint(full_key, (), 0, OWNERS)
    rows_owner = jnp.arange(OWNERS, dtype=jnp.int32)[:, None]
    result = jnp.where(rows_owner == full_owner, PER, base_load - cut_rows)
    return result.astype(jnp.int32)


def plant(array, stream_key, least, top_value):
    shape = array.shape
    place = [jax.random.randint(jax.random.fold_in(stream_key, axis), (), 0, shape[axis]) for axis in range(len(shape))]
    array = array.at[tuple(place)].set(least)
    longest = shape.index(max(shape))
    place[longest] = (place[longest] + 1) % shape[longest]
    return array.at[tuple(place)].set(top_value)


def setup_inputs(seed: int = 0) -> dict:
    keys = jax.random.split(jax.random.key(seed), 6)
    return {
        "record": draw_record(jax.random.fold_in(keys[5], 71), 0),
        "requested": draw_requested(jax.random.fold_in(keys[5], 71), 0),
        "partners": plant(jax.random.randint(keys[2], (OWNERS, 3 * S_DEV, PER), 0, OWNERS * CAP), jax.random.fold_in(keys[2], 1), 0, (OWNERS * CAP) - 1).astype(jnp.int32),
        "codes": plant(jax.random.randint(keys[3], (OWNERS, 3 * S_DEV, PER), 0, 3), jax.random.fold_in(keys[3], 1), 0, 2).astype(jnp.int32),
        "counts": draw_counts(jax.random.fold_in(keys[5], 71), 0),
    }


def reference(record, requested, partners, codes, counts):
    values = record.astype(jnp.float32)
    values = values - lax.optimization_barrier(jnp.mean(values, axis=-1, keepdims=True))
    power_mean = lax.optimization_barrier(jnp.mean(values * values, axis=-1, keepdims=True))
    whitened = (values * lax.rsqrt(power_mean + 1e-06)).astype(jnp.bfloat16)
    fft_len = 2 * WIN
    half_lag = LAGS // 2
    spectra = jnp.fft.rfft(whitened.astype(jnp.float32), n=fft_len, axis=-1)
    flat_spectra = spectra.reshape(STATIONS * 3, WINDOWS, spectra.shape[-1])

    def per_owner(owner_index):
        own_spec = lax.dynamic_slice_in_dim(flat_spectra, owner_index * (S_DEV * 3), S_DEV * 3, 0)
        asked_table = lax.dynamic_index_in_dim(requested, owner_index, axis=0, keepdims=False)
        station_of = (asked_table + jnp.arange(OWNERS, dtype=jnp.int32)[:, None] * S_DEV).reshape(-1)
        slot_ids = lax.dynamic_index_in_dim(partners, owner_index, axis=0, keepdims=False)
        comp_ids = lax.dynamic_index_in_dim(codes, owner_index, axis=0, keepdims=False)
        live_count = lax.dynamic_index_in_dim(counts, owner_index, axis=0, keepdims=False)
        row_ids = (station_of[slot_ids] * 3 + comp_ids).astype(jnp.int32)

        def per_trace(operands):
            own_row, trace_rows, live_n = operands
            partner_spec = flat_spectra[trace_rows]
            cross_spec = lax.optimization_barrier(jnp.sum(jnp.conj(partner_spec) * own_row[None], axis=1))
            lagged = jnp.fft.irfft(cross_spec, n=fft_len, axis=-1)
            picked = jnp.concatenate([lagged[:, fft_len - half_lag:], lagged[:, :LAGS - half_lag]], axis=1)
            live_rows = (jnp.arange(PER, dtype=jnp.int32) < live_n)[:, None]
            return jnp.where(live_rows, picked, 0.0)
        return lax.map(per_trace, (own_spec, row_ids, live_count))
    stacked = lax.map(per_owner, jnp.arange(OWNERS, dtype=jnp.int32))
    stacked = stacked.reshape(OWNERS, 3 * S_DEV * PER, LAGS)
    return (stacked / jnp.sqrt(jnp.float32(WIN * WINDOWS))).astype(jnp.float32)
```

```python
import functools
import math

import jax
import jax.numpy as jnp
from jax import lax
from jax.experimental import pallas as pl
from jax.experimental.pallas import tpu as pltpu
from jax.sharding import PartitionSpec as P

LAGS = 1024


def normalize(traces):
    values = traces.astype(jnp.float32)
    values = values - jnp.mean(values, axis=-1, keepdims=True)
    power_mean = jnp.mean(values * values, axis=-1, keepdims=True)
    return (values * lax.rsqrt(power_mean + 1e-06)).astype(jnp.bfloat16)


def correlate(own_trace, partner_rows, lag_count, block_len):
    window_len = own_trace.shape[0]
    half_lag = lag_count // 2
    padded = jnp.pad(own_trace, (half_lag, half_lag + block_len))
    length = padded.shape[0]
    spread = jnp.broadcast_to(padded, (block_len, length)).reshape(-1)
    spread = jnp.pad(spread, (0, block_len))
    skewed = spread.reshape(block_len, length + 1)[:, : window_len + lag_count]
    hankel = skewed.reshape(block_len, (window_len + lag_count) // block_len, block_len)
    blocks_in = window_len // block_len
    pieces = partner_rows.reshape(partner_rows.shape[0], blocks_in, block_len)
    outputs = []
    for offset in range(lag_count // block_len):
        window_view = hankel[:, offset : offset + blocks_in, :]
        outputs.append(
            jnp.einsum("pmi,imr->pr", pieces, window_view, preferred_element_type=jnp.float32)
        )
    return jnp.concatenate(outputs, axis=1)


def shards(record, requested, partners, codes, counts):
    whitened = normalize(record)
    local_stations, comp_count, window_count, window_len = whitened.shape
    owners = lax.axis_size("pairs")
    capacity = requested.shape[2]
    per_trace = partners.shape[2]
    trace_count = local_stations * comp_count
    block_len = math.gcd(math.gcd(128, window_len), LAGS)
    own_index = lax.axis_index("pairs")
    slot_ids = partners[0]
    comp_ids = codes[0]
    everyone = lax.all_gather(whitened, "pairs", axis=0, tiled=True)
    trace_pool = everyone.reshape(owners * local_stations * comp_count, window_count, window_len)
    asked_table = lax.dynamic_index_in_dim(requested, own_index, axis=0, keepdims=False)
    station_of = (
        asked_table + jnp.arange(owners, dtype=jnp.int32)[:, None] * local_stations
    ).reshape(-1)
    matches = slot_ids[:, :, None] == jnp.arange(owners * capacity, dtype=jnp.int32)[None, None, :]
    stations = jnp.sum(jnp.where(matches, station_of[None, None, :], 0), axis=-1)
    row_ids = stations * comp_count + comp_ids
    picked = jnp.take(trace_pool, row_ids.reshape(-1), axis=0)
    live_rows = jnp.arange(per_trace, dtype=jnp.int32)[None, :] < counts[0][:, None]
    picked = jnp.where(live_rows.reshape(-1)[:, None, None], picked, jnp.zeros((), jnp.bfloat16))
    picked = picked.reshape(trace_count, per_trace, window_count, window_len)
    picked = jnp.moveaxis(picked, 2, 1).reshape(trace_count * window_count, per_trace, window_len)
    own_rows = whitened.reshape(trace_count * window_count, window_len)

    def one_trace(operands):
        own_row, partner_rows = operands
        return correlate(own_row, partner_rows, LAGS, block_len)

    lagged = lax.map(one_trace, (own_rows, picked))
    lagged = lagged.reshape(trace_count, window_count, per_trace, LAGS)
    total_windows = window_count * lax.axis_size("tm")
    window_term = jnp.sum(lagged, axis=1) * (1.0 / math.sqrt(window_len * total_windows))
    window_term = window_term.reshape(1, trace_count * per_trace, LAGS)
    return lax.psum_scatter(window_term, "tm", scatter_dimension=1, tiled=True)


MESH = pl.DeviceIdType.MESH
HALF = 128
BLOCK = 2 * HALF
FROM_X, FROM_Y, DIAG_A, DIAG_B, CORE_OWN, CORE_X, CORE_Y, CORE_D = range(8)


def xor_step(t, k):
    if k == 1:
        return t + 1 - 2 * lax.rem(t, 2)
    if k == 2:
        return lax.rem(t + 2, 4)
    return 3 - t


def exchange_kernel(
    dims, asked_ref, record_ref, cc_ref, *scratch
):
    traces, blocks_in, owners, capacity, comps, own_count, lag_blocks = dims
    blks = scratch[:4]
    (rows32, pool32, own32, lhs, hankel, acc, send, recv, zsend, zrecv) = scratch[4:]
    pool = owners * capacity * comps
    first_s, last_s = 1, blocks_in + lag_blocks - 3
    t = lax.axis_index("tm")
    e = lax.axis_index("pairs")
    core, x, y = lax.rem(e, 2), lax.rem(e // 2, 2), e // 4
    ex, ey, ec = e + 2 - 4 * x, e + 4 - 8 * y, e + 1 - 2 * core
    ed = ex + 4 - 8 * y
    cx, cy, cd = ex + 1 - 2 * core, ey + 1 - 2 * core, ed + 1 - 2 * core

    barrier = pltpu.get_barrier_semaphore()
    for peer in ((t, ex), (t, ey), (t, ec)) + tuple((xor_step(t, k), e) for k in (1, 2, 3)):
        pl.semaphore_signal(barrier, inc=1, device_id=peer, device_id_type=MESH)

    row_index = lax.broadcasted_iota(jnp.int32, (HALF, HALF), 0)
    lane_index = lax.broadcasted_iota(jnp.int32, (HALF, HALF), 1)
    mirror = jnp.where(row_index + lane_index == HALF - 1, 1.0, 0.0).astype(jnp.bfloat16)

    def flip_halves(tile):
        return jnp.dot(tile, mirror, preferred_element_type=jnp.float32)

    values = record_ref[...].astype(jnp.float32)
    values = values - jnp.mean(values, axis=-1, keepdims=True)
    power_mean = jnp.mean(values * values, axis=-1, keepdims=True)
    values = values * lax.rsqrt(power_mean + 1e-06)
    for m in range(blocks_in):
        for h in (0, 1):
            lane = m * BLOCK + h * HALF
            rows32[h, pl.ds(m, traces, stride=blocks_in), :] = values[:, lane : lane + HALF]
    for h in (0, 1):
        blks[0][e, :, :, h * HALF : (h + 1) * HALF] = (
            flip_halves(rows32[h].astype(jnp.bfloat16))
            .astype(jnp.bfloat16)
            .reshape(traces, blocks_in, HALF)
        )
    pl.semaphore_wait(barrier, 6)

    def plane_copy(k, kind, origin, target):
        blk = blks[k]
        if kind == DIAG_A:
            ref = blk.at[origin, pl.ds(0, traces // 2)]
        elif kind == DIAG_B:
            ref = blk.at[origin, pl.ds(traces // 2, traces // 2)]
        else:
            ref = blk.at[origin]
        return pltpu.make_async_remote_copy(
            src_ref=ref, dst_ref=ref,
            send_sem=send.at[k, kind], recv_sem=recv.at[k, kind],
            device_id=(t, target), device_id_type=MESH,
        )

    def z_copy(k):
        return pltpu.make_async_remote_copy(
            src_ref=blks[0].at[e], dst_ref=blks[k].at[e],
            send_sem=zsend.at[k - 1], recv_sem=zrecv.at[k - 1],
            device_id=(xor_step(t, k), e), device_id_type=MESH,
        )

    def send_own(k):
        plane_copy(k, FROM_X, e, ex).start()
        plane_copy(k, FROM_Y, e, ey).start()
        plane_copy(k, CORE_OWN, e, ec).start()

    def forward_xy(k):
        plane_copy(k, FROM_X, ex, ex).wait_recv()
        plane_copy(k, DIAG_A, ex, ey).start()
        plane_copy(k, CORE_X, ex, ec).start()
        plane_copy(k, FROM_Y, ey, ey).wait_recv()
        plane_copy(k, DIAG_B, ey, ex).start()
        plane_copy(k, CORE_Y, ey, ec).start()

    def forward_diag(k):
        plane_copy(k, DIAG_A, ed, ey).wait_recv()
        plane_copy(k, DIAG_B, ed, ex).wait_recv()
        plane_copy(k, CORE_D, ed, ec).start()

    def wait_core(k):
        plane_copy(k, CORE_OWN, ec, ec).wait_recv()
        plane_copy(k, CORE_X, cx, ec).wait_recv()
        plane_copy(k, CORE_Y, cy, ec).wait_recv()
        plane_copy(k, CORE_D, cd, ec).wait_recv()

    below = lane_index <= row_index
    zeros = jnp.zeros((HALF, HALF), jnp.float32)

    def put(j, s, row_half, lane_half, tile):
        if first_s <= s <= last_s:
            row = (s - first_s) * BLOCK + row_half * HALF
            hankel[j, row : row + HALF, lane_half * HALF : (lane_half + 1) * HALF] = tile

    def build(k):
        def one(j, carry):
            for h in (0, 1):
                lanes = slice(h * HALF, (h + 1) * HALF)
                own32[:, lanes] = flip_halves(blks[k][e, own_count * t + j, :, lanes])
            before = zeros
            for c in range(2 * blocks_in + 1):
                if c < 2 * blocks_in:
                    half = c % 2
                    row = own32[c // 2 : c // 2 + 1, half * HALF : (half + 1) * HALF]
                    now = pltpu.roll(
                        jnp.broadcast_to(row, (HALF, HALF)), 1, 1, stride=1, stride_axis=0
                    )
                else:
                    now = zeros
                tile = jnp.where(below, before, now).astype(jnp.bfloat16)
                before = now
                chunk = c + lag_blocks - 1
                s = chunk // 2
                if chunk % 2:
                    put(j, s, 0, 1, tile)
                    put(j, s, 1, 0, tile)
                else:
                    put(j, s, 0, 0, tile)
                    put(j, s - 1, 1, 1, tile)
            return carry

        lax.fori_loop(0, own_count, one, 0)

    def correlate_window(k):
        blk = blks[k]
        for d in range(owners):
            for i in range(capacity):
                station = asked_ref[e, d, i]
                slot = (d * capacity + i) * comps * blocks_in
                station_rows = (
                    blk[d, pl.ds(station * comps, comps)]
                    .astype(jnp.float32)
                    .reshape(comps * blocks_in, BLOCK)
                )
                for h in (0, 1):
                    pool32[h, slot : slot + comps * blocks_in, :] = station_rows[
                        :, h * HALF : (h + 1) * HALF
                    ]
        for m in range(blocks_in):
            for h in (0, 1):
                part = pool32[h, pl.ds(m, pool, stride=blocks_in), :].astype(jnp.bfloat16)
                for q in range(lag_blocks):
                    s = m + q
                    if first_s <= s <= last_s:
                        col = (s - first_s) * BLOCK + h * HALF
                        row = (lag_blocks - 1 - q) * pool
                        lhs[row : row + pool, col : col + HALF] = part

        def one(j, carry):
            term = jnp.dot(lhs[...], hankel[j], preferred_element_type=jnp.float32)
            if k == 0:
                acc[j] = term
            else:
                acc[j] += term
            return carry

        lax.fori_loop(0, own_count, one, 0)

    for k in (1, 2, 3):
        z_copy(k).start()
    send_own(0)
    for q in range(lag_blocks):
        for s in range(first_s, last_s + 1):
            if not 0 <= s - (lag_blocks - 1) + q < blocks_in:
                col = (s - first_s) * BLOCK
                lhs[q * pool : (q + 1) * pool, col : col + BLOCK] = jnp.zeros((pool, BLOCK), jnp.bfloat16)
    for j in range(own_count):
        put(j, first_s, 0, 0, zeros.astype(jnp.bfloat16))
        put(j, last_s, 1, 1, zeros.astype(jnp.bfloat16))

    build(0)
    z_copy(1).wait_recv()
    send_own(1)
    forward_xy(0)
    z_copy(2).wait_recv()
    send_own(2)
    forward_diag(0)
    forward_xy(1)
    wait_core(0)
    correlate_window(0)
    z_copy(3).wait_recv()
    send_own(3)
    forward_diag(1)
    forward_xy(2)
    build(1)
    wait_core(1)
    correlate_window(1)
    forward_diag(2)
    forward_xy(3)
    build(2)
    wait_core(2)
    correlate_window(2)
    forward_diag(3)
    build(3)
    wait_core(3)
    correlate_window(3)
    cc_ref[...] = acc[...]

    for k in (1, 2, 3):
        z_copy(k).wait_send()
    for k in range(4):
        plane_copy(k, FROM_X, e, ex).wait_send()
        plane_copy(k, FROM_Y, e, ey).wait_send()
        plane_copy(k, CORE_OWN, e, ec).wait_send()
        plane_copy(k, DIAG_A, ex, ey).wait_send()
        plane_copy(k, CORE_X, ex, ec).wait_send()
        plane_copy(k, DIAG_B, ey, ex).wait_send()
        plane_copy(k, CORE_Y, ey, ec).wait_send()
        plane_copy(k, CORE_D, ed, ec).wait_send()


def select_kernel(scale, own_count, comps, lag_blocks, counts_ref, partners_ref, codes_ref, cc_ref, out_ref):
    t = lax.axis_index("tm")
    pool = cc_ref.shape[1] // lag_blocks
    slots = partners_ref.shape[2]
    pool_row = lax.broadcasted_iota(jnp.int32, (pool, slots), 0)
    slot_lane = lax.broadcasted_iota(jnp.int32, (pool, slots), 1)
    dims = (((0,), (0,)), ((), ()))
    for j in range(own_count):
        trace = own_count * t + j
        wanted = partners_ref[0, pl.ds(trace, 1), :] * comps + codes_ref[0, pl.ds(trace, 1), :]
        hit = (wanted == pool_row) & (slot_lane < counts_ref[0, trace])
        chosen = jnp.where(hit, 1.0, 0.0).astype(jnp.bfloat16)
        for q in range(lag_blocks):
            part = cc_ref[j, q * pool : (q + 1) * pool, :]
            high = part.astype(jnp.bfloat16)
            rest = part - high.astype(jnp.float32)
            middle = rest.astype(jnp.bfloat16)
            low = (rest - middle.astype(jnp.float32)).astype(jnp.bfloat16)
            total = lax.dot_general(chosen, low, dims, preferred_element_type=jnp.float32)
            total += lax.dot_general(chosen, middle, dims, preferred_element_type=jnp.float32)
            total += lax.dot_general(chosen, high, dims, preferred_element_type=jnp.float32)
            lag = (lag_blocks - 1 - q) * BLOCK
            out_ref[0, j * slots : (j + 1) * slots, lag : lag + BLOCK] = total * scale


def gathered_shards(record, requested, partners, codes, counts):
    stations, comps, _, window_len = record.shape
    owners, capacity = requested.shape[1:]
    traces = stations * comps
    windows = lax.axis_size("tm")
    own_count = traces // windows
    blocks_in, lag_blocks = window_len // BLOCK, LAGS // BLOCK
    pool = owners * capacity * comps
    depth = (blocks_in + lag_blocks - 3) * BLOCK
    slots = partners.shape[2]
    cc_shape = jax.ShapeDtypeStruct((own_count, lag_blocks * pool, BLOCK), jnp.float32)
    dims = (traces, blocks_in, owners, capacity, comps, own_count, lag_blocks)
    vmem = pl.BlockSpec(memory_space=pltpu.VMEM)
    smem = pl.BlockSpec(memory_space=pltpu.SMEM)
    cc = pl.pallas_call(
        functools.partial(exchange_kernel, dims),
        out_shape=cc_shape,
        in_specs=[smem, vmem],
        out_specs=vmem,
        scratch_shapes=[pltpu.VMEM((owners, traces, blocks_in, BLOCK), jnp.bfloat16)] * 4
        + [
            pltpu.VMEM((2, traces * blocks_in, HALF), jnp.float32),
            pltpu.VMEM((2, pool * blocks_in, HALF), jnp.float32),
            pltpu.VMEM((blocks_in, BLOCK), jnp.float32),
            pltpu.VMEM((lag_blocks * pool, depth), jnp.bfloat16),
            pltpu.VMEM((own_count, depth, BLOCK), jnp.bfloat16),
            pltpu.VMEM(cc_shape.shape, jnp.float32),
            pltpu.SemaphoreType.DMA((4, 8)),
            pltpu.SemaphoreType.DMA((4, 8)),
            pltpu.SemaphoreType.DMA((3,)),
            pltpu.SemaphoreType.DMA((3,)),
        ],
        compiler_params=pltpu.CompilerParams(
            collective_id=0, has_side_effects=True, vmem_limit_bytes=40 * 1024 * 1024
        ),
    )(requested, record.reshape(traces, window_len))
    return pl.pallas_call(
        functools.partial(
            select_kernel, 1.0 / math.sqrt(window_len * windows), own_count, comps, lag_blocks
        ),
        out_shape=jax.ShapeDtypeStruct((1, own_count * slots, LAGS), jnp.float32),
        in_specs=[smem, vmem, vmem, vmem],
        out_specs=vmem,
        compiler_params=pltpu.CompilerParams(vmem_limit_bytes=16 * 1024 * 1024),
    )(counts, partners, codes, cc)


def solution(mesh):
    def body(record, requested, partners, codes, counts):
        planes = lax.axis_size("tm") == 4 and lax.axis_size("pairs") == 8
        stations, comps, window_count, window_len = record.shape
        fits = (
            window_count == 1
            and stations == 4
            and window_len % BLOCK == 0
            and LAGS == 4 * BLOCK
        )
        form = gathered_shards if planes and fits else shards
        return form(record, requested, partners, codes, counts)

    return jax.shard_map(
        body,
        mesh=mesh,
        in_specs=(
            P("pairs", None, "tm", None),
            P(),
            P("pairs", None, None),
            P("pairs", None, None),
            P("pairs", None),
        ),
        out_specs=P("pairs", "tm", None),
        check_vma=False,
    )
```

```python
import functools
import math

import jax
import jax.numpy as jnp
from jax import lax
from jax.experimental import pallas as pl
from jax.experimental.pallas import tpu as pltpu
from jax.sharding import PartitionSpec as P

LAGS = 1024


def normalize(traces):
    values = traces.astype(jnp.float32)
    values = values - jnp.mean(values, axis=-1, keepdims=True)
    power_mean = jnp.mean(values * values, axis=-1, keepdims=True)
    return (values * lax.rsqrt(power_mean + 1e-06)).astype(jnp.bfloat16)


def correlate(own_trace, partner_rows, lag_count, block_len):
    window_len = own_trace.shape[0]
    half_lag = lag_count // 2
    padded = jnp.pad(own_trace, (half_lag, half_lag + block_len))
    length = padded.shape[0]
    spread = jnp.broadcast_to(padded, (block_len, length)).reshape(-1)
    spread = jnp.pad(spread, (0, block_len))
    skewed = spread.reshape(block_len, length + 1)[:, : window_len + lag_count]
    hankel = skewed.reshape(block_len, (window_len + lag_count) // block_len, block_len)
    blocks_in = window_len // block_len
    pieces = partner_rows.reshape(partner_rows.shape[0], blocks_in, block_len)
    outputs = []
    for offset in range(lag_count // block_len):
        window_view = hankel[:, offset : offset + blocks_in, :]
        outputs.append(
            jnp.einsum("pmi,imr->pr", pieces, window_view, preferred_element_type=jnp.float32)
        )
    return jnp.concatenate(outputs, axis=1)


def shards(record, requested, partners, codes, counts):
    whitened = normalize(record)
    local_stations, comp_count, window_count, window_len = whitened.shape
    owners = lax.axis_size("pairs")
    capacity = requested.shape[2]
    per_trace = partners.shape[2]
    trace_count = local_stations * comp_count
    block_len = math.gcd(math.gcd(128, window_len), LAGS)
    own_index = lax.axis_index("pairs")
    slot_ids = partners[0]
    comp_ids = codes[0]
    everyone = lax.all_gather(whitened, "pairs", axis=0, tiled=True)
    trace_pool = everyone.reshape(owners * local_stations * comp_count, window_count, window_len)
    asked_table = lax.dynamic_index_in_dim(requested, own_index, axis=0, keepdims=False)
    station_of = (
        asked_table + jnp.arange(owners, dtype=jnp.int32)[:, None] * local_stations
    ).reshape(-1)
    matches = slot_ids[:, :, None] == jnp.arange(owners * capacity, dtype=jnp.int32)[None, None, :]
    stations = jnp.sum(jnp.where(matches, station_of[None, None, :], 0), axis=-1)
    row_ids = stations * comp_count + comp_ids
    picked = jnp.take(trace_pool, row_ids.reshape(-1), axis=0)
    live_rows = jnp.arange(per_trace, dtype=jnp.int32)[None, :] < counts[0][:, None]
    picked = jnp.where(live_rows.reshape(-1)[:, None, None], picked, jnp.zeros((), jnp.bfloat16))
    picked = picked.reshape(trace_count, per_trace, window_count, window_len)
    picked = jnp.moveaxis(picked, 2, 1).reshape(trace_count * window_count, per_trace, window_len)
    own_rows = whitened.reshape(trace_count * window_count, window_len)

    def one_trace(operands):
        own_row, partner_rows = operands
        return correlate(own_row, partner_rows, LAGS, block_len)

    lagged = lax.map(one_trace, (own_rows, picked))
    lagged = lagged.reshape(trace_count, window_count, per_trace, LAGS)
    total_windows = window_count * lax.axis_size("tm")
    window_term = jnp.sum(lagged, axis=1) * (1.0 / math.sqrt(window_len * total_windows))
    window_term = window_term.reshape(1, trace_count * per_trace, LAGS)
    return lax.psum_scatter(window_term, "tm", scatter_dimension=1, tiled=True)


MESH = pl.DeviceIdType.MESH
HALF = 128
BLOCK = 2 * HALF
FROM_X, FROM_Y, DIAG_A, DIAG_B, CORE_OWN, CORE_X, CORE_Y, CORE_D = range(8)


def xor_step(t, k):
    if k == 1:
        return t + 1 - 2 * lax.rem(t, 2)
    if k == 2:
        return lax.rem(t + 2, 4)
    return 3 - t


def exchange_kernel(
    dims, asked_ref, record_ref, cc_ref, *scratch
):
    traces, blocks_in, owners, capacity, comps, own_count, lag_blocks = dims
    blks = scratch[:4]
    (rows32, pool32, own32, pool16, hankel, send, recv, zsend, zrecv) = scratch[4:]
    pool = owners * capacity * comps
    first_s, last_s = 1, blocks_in + lag_blocks - 3
    t = lax.axis_index("tm")
    e = lax.axis_index("pairs")
    core, x, y = lax.rem(e, 2), lax.rem(e // 2, 2), e // 4
    ex, ey, ec = e + 2 - 4 * x, e + 4 - 8 * y, e + 1 - 2 * core
    ed = ex + 4 - 8 * y
    cx, cy, cd = ex + 1 - 2 * core, ey + 1 - 2 * core, ed + 1 - 2 * core

    barrier = pltpu.get_barrier_semaphore()
    for peer in ((t, ex), (t, ey), (t, ec)) + tuple((xor_step(t, k), e) for k in (1, 2, 3)):
        pl.semaphore_signal(barrier, inc=1, device_id=peer, device_id_type=MESH)

    row_index = lax.broadcasted_iota(jnp.int32, (HALF, HALF), 0)
    lane_index = lax.broadcasted_iota(jnp.int32, (HALF, HALF), 1)
    mirror = jnp.where(row_index + lane_index == HALF - 1, 1.0, 0.0).astype(jnp.bfloat16)

    def flip_halves(tile):
        return jnp.dot(tile, mirror, preferred_element_type=jnp.float32)

    stations = traces // comps
    for comp in range(comps):
        values = record_ref[comp].astype(jnp.float32)
        values = values - jnp.mean(values, axis=-1, keepdims=True)
        power_mean = jnp.mean(values * values, axis=-1, keepdims=True)
        values = values * lax.rsqrt(power_mean + 1e-06)
        for m in range(blocks_in):
            rows = pl.ds(comp * blocks_in + m, stations, stride=comps * blocks_in)
            for h in (0, 1):
                lane = m * BLOCK + h * HALF
                rows32[h, rows, :] = values[:, lane : lane + HALF]
    for h in (0, 1):
        blks[0][e, :, :, h * HALF : (h + 1) * HALF] = (
            flip_halves(rows32[h].astype(jnp.bfloat16))
            .astype(jnp.bfloat16)
            .reshape(traces, blocks_in, HALF)
        )
    pl.semaphore_wait(barrier, 6)

    def plane_copy(k, kind, origin, target):
        blk = blks[k]
        if kind == DIAG_A:
            ref = blk.at[origin, pl.ds(0, traces // 2)]
        elif kind == DIAG_B:
            ref = blk.at[origin, pl.ds(traces // 2, traces // 2)]
        else:
            ref = blk.at[origin]
        return pltpu.make_async_remote_copy(
            src_ref=ref, dst_ref=ref,
            send_sem=send.at[k, kind], recv_sem=recv.at[k, kind],
            device_id=(t, target), device_id_type=MESH,
        )

    def z_copy(k):
        return pltpu.make_async_remote_copy(
            src_ref=blks[0].at[e], dst_ref=blks[k].at[e],
            send_sem=zsend.at[k - 1], recv_sem=zrecv.at[k - 1],
            device_id=(xor_step(t, k), e), device_id_type=MESH,
        )

    def send_own(k):
        plane_copy(k, FROM_X, e, ex).start()
        plane_copy(k, FROM_Y, e, ey).start()
        plane_copy(k, CORE_OWN, e, ec).start()

    def forward_xy(k):
        plane_copy(k, FROM_X, ex, ex).wait_recv()
        plane_copy(k, DIAG_A, ex, ey).start()
        plane_copy(k, CORE_X, ex, ec).start()
        plane_copy(k, FROM_Y, ey, ey).wait_recv()
        plane_copy(k, DIAG_B, ey, ex).start()
        plane_copy(k, CORE_Y, ey, ec).start()

    def forward_diag(k):
        plane_copy(k, DIAG_A, ed, ey).wait_recv()
        plane_copy(k, DIAG_B, ed, ex).wait_recv()
        plane_copy(k, CORE_D, ed, ec).start()

    def wait_core(k):
        plane_copy(k, CORE_OWN, ec, ec).wait_recv()
        plane_copy(k, CORE_X, cx, ec).wait_recv()
        plane_copy(k, CORE_Y, cy, ec).wait_recv()
        plane_copy(k, CORE_D, cd, ec).wait_recv()

    below = lane_index <= row_index
    nothing = jnp.zeros((HALF, HALF), jnp.bfloat16)
    first_chunk = 2 * first_s

    def put(k, j, chunk, tile):
        lane = (chunk - first_chunk) * HALF
        hankel[own_count * k + j, :, lane : lane + HALF] = tile

    def build(k):
        def one(j, carry):
            for h in (0, 1):
                lanes = slice(h * HALF, (h + 1) * HALF)
                own32[:, lanes] = flip_halves(blks[k][e, own_count * t + j, :, lanes])
            before = nothing
            for c in range(2 * blocks_in + 1):
                if c < 2 * blocks_in:
                    half = c % 2
                    row = own32[c // 2 : c // 2 + 1, half * HALF : (half + 1) * HALF]
                    skewed = pltpu.roll(
                        jnp.broadcast_to(row, (16, HALF)), 1, 1, stride=1, stride_axis=0
                    ).astype(jnp.bfloat16)
                    now = jnp.concatenate(
                        [skewed] + [pltpu.roll(skewed, 16 * a, 1) for a in range(1, HALF // 16)], axis=0
                    )
                else:
                    now = nothing
                put(k, j, c + lag_blocks - 1, jnp.where(below, before, now))
                before = now
            return carry

        lax.fori_loop(0, own_count, one, 0)

    def correlate_window(k):
        blk = blks[k]
        for d in range(owners):
            for i in range(capacity):
                station = asked_ref[e, i, d]
                slot = (d * capacity + i) * comps * blocks_in
                station_rows = (
                    blk[d, pl.ds(station * comps, comps)]
                    .astype(jnp.float32)
                    .reshape(comps * blocks_in, BLOCK)
                )
                for h in (0, 1):
                    pool32[h, slot : slot + comps * blocks_in, :] = station_rows[
                        :, h * HALF : (h + 1) * HALF
                    ]
        for m in range(blocks_in):
            for h in (0, 1):
                part = pool32[h, pl.ds(m, pool, stride=blocks_in), :].astype(jnp.bfloat16)
                pool16[m, :, h * HALF : (h + 1) * HALF] = part

        def one(j, carry):
            empty = jnp.zeros((pool, BLOCK), jnp.bfloat16)
            left = jnp.concatenate(
                [
                    jnp.concatenate(
                        [
                            pool16[s - q] if 0 <= s - q < blocks_in else empty
                            for s in range(first_s, last_s + 1)
                        ],
                        axis=1,
                    )
                    for q in reversed(range(lag_blocks))
                ],
                axis=0,
            )
            index = own_count * k + j
            right = jnp.concatenate(
                [
                    hankel[index, :, lane : lane + BLOCK]
                    for s in range(first_s, last_s + 1)
                    for lane in ((2 * s - first_chunk) * HALF, (2 * s + 1 - first_chunk) * HALF)
                ],
                axis=0,
            )
            term = jnp.dot(left, right, preferred_element_type=jnp.float32)
            if k == 0:
                cc_ref[j] = term
            else:
                cc_ref[j] += term
            return carry

        lax.fori_loop(0, own_count, one, 0)

    for k in (1, 2, 3):
        z_copy(k).start()
    send_own(0)
    for k in range(4):
        for j in range(own_count):
            put(k, j, first_chunk, nothing)
            put(k, j, 2 * last_s + 2, nothing)

    build(0)
    z_copy(1).wait_recv()
    send_own(1)
    build(1)
    forward_xy(0)
    z_copy(2).wait_recv()
    send_own(2)
    build(2)
    forward_diag(0)
    forward_xy(1)
    z_copy(3).wait_recv()
    send_own(3)
    wait_core(0)
    correlate_window(0)
    forward_diag(1)
    forward_xy(2)
    build(3)
    wait_core(1)
    correlate_window(1)
    forward_diag(2)
    forward_xy(3)
    wait_core(2)
    correlate_window(2)
    forward_diag(3)
    wait_core(3)
    correlate_window(3)

    for k in (1, 2, 3):
        z_copy(k).wait_send()
    for k in range(4):
        plane_copy(k, FROM_X, e, ex).wait_send()
        plane_copy(k, FROM_Y, e, ey).wait_send()
        plane_copy(k, CORE_OWN, e, ec).wait_send()
        plane_copy(k, DIAG_A, ex, ey).wait_send()
        plane_copy(k, CORE_X, ex, ec).wait_send()
        plane_copy(k, DIAG_B, ey, ex).wait_send()
        plane_copy(k, CORE_Y, ey, ec).wait_send()
        plane_copy(k, CORE_D, ed, ec).wait_send()


def select_kernel(scale, own_count, comps, lag_blocks, counts_ref, partners_ref, codes_ref, cc_ref, out_ref):
    t = lax.axis_index("tm")
    pool = cc_ref.shape[1] // lag_blocks
    slots = partners_ref.shape[2]
    pool_row = lax.broadcasted_iota(jnp.int32, (pool, slots), 0)
    slot_lane = lax.broadcasted_iota(jnp.int32, (pool, slots), 1)
    dims = (((0,), (0,)), ((), ()))
    for j in range(own_count):
        trace = own_count * t + j
        wanted = partners_ref[trace] * comps + codes_ref[trace]
        hit = (wanted == pool_row) & (slot_lane < counts_ref[0, trace])
        chosen = jnp.where(hit, 1.0, 0.0).astype(jnp.bfloat16)
        for q in range(lag_blocks):
            part = cc_ref[j, q * pool : (q + 1) * pool, :]
            high = part.astype(jnp.bfloat16)
            rest = part - high.astype(jnp.float32)
            middle = rest.astype(jnp.bfloat16)
            low = (rest - middle.astype(jnp.float32)).astype(jnp.bfloat16)
            total = lax.dot_general(chosen, low, dims, preferred_element_type=jnp.float32)
            total += lax.dot_general(chosen, middle, dims, preferred_element_type=jnp.float32)
            total += lax.dot_general(chosen, high, dims, preferred_element_type=jnp.float32)
            lag = (lag_blocks - 1 - q) * BLOCK
            out_ref[0, j * slots : (j + 1) * slots, lag : lag + BLOCK] = total * scale


def gathered_shards(record, requested, partners, codes, counts):
    stations, comps, _, window_len = record.shape
    owners, capacity = requested.shape[1:]
    traces = stations * comps
    windows = lax.axis_size("tm")
    own_count = traces // windows
    blocks_in, lag_blocks = window_len // BLOCK, LAGS // BLOCK
    pool = owners * capacity * comps
    depth = (blocks_in + lag_blocks - 3) * BLOCK
    slots = partners.shape[2]
    cc_shape = jax.ShapeDtypeStruct((own_count, lag_blocks * pool, BLOCK), jnp.float32)
    dims = (traces, blocks_in, owners, capacity, comps, own_count, lag_blocks)
    vmem = pl.BlockSpec(memory_space=pltpu.VMEM)
    smem = pl.BlockSpec(memory_space=pltpu.SMEM)
    cc = pl.pallas_call(
        functools.partial(exchange_kernel, dims),
        out_shape=cc_shape,
        in_specs=[smem, vmem],
        out_specs=vmem,
        scratch_shapes=[pltpu.VMEM((owners, traces, blocks_in, BLOCK), jnp.bfloat16)] * 4
        + [
            pltpu.VMEM((2, traces * blocks_in, HALF), jnp.float32),
            pltpu.VMEM((2, pool * blocks_in, HALF), jnp.float32),
            pltpu.VMEM((blocks_in, BLOCK), jnp.float32),
            pltpu.VMEM((blocks_in, pool, BLOCK), jnp.bfloat16),
            pltpu.VMEM((4 * own_count, HALF, depth + HALF), jnp.bfloat16),
            pltpu.SemaphoreType.DMA((4, 8)),
            pltpu.SemaphoreType.DMA((4, 8)),
            pltpu.SemaphoreType.DMA((3,)),
            pltpu.SemaphoreType.DMA((3,)),
        ],
        compiler_params=pltpu.CompilerParams(
            collective_id=0, has_side_effects=True, vmem_limit_bytes=40 * 1024 * 1024
        ),
    )(requested.transpose(0, 2, 1), record.transpose(2, 1, 0, 3)[0])
    return pl.pallas_call(
        functools.partial(
            select_kernel, 1.0 / math.sqrt(window_len * windows), own_count, comps, lag_blocks
        ),
        out_shape=jax.ShapeDtypeStruct((1, own_count * slots, LAGS), jnp.float32),
        in_specs=[smem, vmem, vmem, vmem],
        out_specs=vmem,
        compiler_params=pltpu.CompilerParams(vmem_limit_bytes=16 * 1024 * 1024),
    )(counts, partners.transpose(1, 0, 2), codes.transpose(1, 0, 2), cc)


def solution(mesh):
    def body(record, requested, partners, codes, counts):
        planes = lax.axis_size("tm") == 4 and lax.axis_size("pairs") == 8
        stations, comps, window_count, window_len = record.shape
        fits = (
            window_count == 1
            and stations == 4
            and window_len % BLOCK == 0
            and LAGS == 4 * BLOCK
        )
        form = gathered_shards if planes and fits else shards
        return form(record, requested, partners, codes, counts)

    return jax.shard_map(
        body,
        mesh=mesh,
        in_specs=(
            P("pairs", None, "tm", None),
            P(),
            P("pairs", None, None),
            P("pairs", None, None),
            P("pairs", None),
        ),
        out_specs=P("pairs", "tm", None),
        check_vma=False,
    )
```

```python
import functools
import math

import jax
import jax.numpy as jnp
from jax import lax
from jax.experimental import pallas as pl
from jax.experimental.pallas import tpu as pltpu
from jax.sharding import PartitionSpec as P

LAGS = 1024


def normalize(traces):
    values = traces.astype(jnp.float32)
    values = values - jnp.mean(values, axis=-1, keepdims=True)
    power_mean = jnp.mean(values * values, axis=-1, keepdims=True)
    return (values * lax.rsqrt(power_mean + 1e-06)).astype(jnp.bfloat16)


def correlate(own_trace, partner_rows, lag_count, block_len):
    window_len = own_trace.shape[0]
    half_lag = lag_count // 2
    padded = jnp.pad(own_trace, (half_lag, half_lag + block_len))
    length = padded.shape[0]
    spread = jnp.broadcast_to(padded, (block_len, length)).reshape(-1)
    spread = jnp.pad(spread, (0, block_len))
    skewed = spread.reshape(block_len, length + 1)[:, : window_len + lag_count]
    hankel = skewed.reshape(block_len, (window_len + lag_count) // block_len, block_len)
    blocks_in = window_len // block_len
    pieces = partner_rows.reshape(partner_rows.shape[0], blocks_in, block_len)
    outputs = []
    for offset in range(lag_count // block_len):
        window_view = hankel[:, offset : offset + blocks_in, :]
        outputs.append(
            jnp.einsum("pmi,imr->pr", pieces, window_view, preferred_element_type=jnp.float32)
        )
    return jnp.concatenate(outputs, axis=1)


def shards(record, requested, partners, codes, counts):
    whitened = normalize(record)
    local_stations, comp_count, window_count, window_len = whitened.shape
    owners = lax.axis_size("pairs")
    capacity = requested.shape[2]
    per_trace = partners.shape[2]
    trace_count = local_stations * comp_count
    block_len = math.gcd(math.gcd(128, window_len), LAGS)
    own_index = lax.axis_index("pairs")
    slot_ids = partners[0]
    comp_ids = codes[0]
    everyone = lax.all_gather(whitened, "pairs", axis=0, tiled=True)
    trace_pool = everyone.reshape(owners * local_stations * comp_count, window_count, window_len)
    asked_table = lax.dynamic_index_in_dim(requested, own_index, axis=0, keepdims=False)
    station_of = (
        asked_table + jnp.arange(owners, dtype=jnp.int32)[:, None] * local_stations
    ).reshape(-1)
    matches = slot_ids[:, :, None] == jnp.arange(owners * capacity, dtype=jnp.int32)[None, None, :]
    stations = jnp.sum(jnp.where(matches, station_of[None, None, :], 0), axis=-1)
    row_ids = stations * comp_count + comp_ids
    picked = jnp.take(trace_pool, row_ids.reshape(-1), axis=0)
    live_rows = jnp.arange(per_trace, dtype=jnp.int32)[None, :] < counts[0][:, None]
    picked = jnp.where(live_rows.reshape(-1)[:, None, None], picked, jnp.zeros((), jnp.bfloat16))
    picked = picked.reshape(trace_count, per_trace, window_count, window_len)
    picked = jnp.moveaxis(picked, 2, 1).reshape(trace_count * window_count, per_trace, window_len)
    own_rows = whitened.reshape(trace_count * window_count, window_len)

    def one_trace(operands):
        own_row, partner_rows = operands
        return correlate(own_row, partner_rows, LAGS, block_len)

    lagged = lax.map(one_trace, (own_rows, picked))
    lagged = lagged.reshape(trace_count, window_count, per_trace, LAGS)
    total_windows = window_count * lax.axis_size("tm")
    window_term = jnp.sum(lagged, axis=1) * (1.0 / math.sqrt(window_len * total_windows))
    window_term = window_term.reshape(1, trace_count * per_trace, LAGS)
    return lax.psum_scatter(window_term, "tm", scatter_dimension=1, tiled=True)


MESH = pl.DeviceIdType.MESH
HALF = 128
BLOCK = 2 * HALF
FROM_X, FROM_Y, DIAG_A, DIAG_B, CORE_OWN, CORE_X, CORE_Y, CORE_D = range(8)


def exchange_kernel(
    dims, asked_hbm, record_hbm, cc_ref, *scratch
):
    traces, blocks_in, owners, capacity, comps, own_count, lag_blocks = dims
    blks = scratch[:4]
    (asked_ref, record_ref, rows32, pool32, own32, pool16, hankel) = scratch[4:11]
    (send, recv, zsend, zrecv, local) = scratch[11:]
    pool = owners * capacity * comps
    first_s, last_s = 1, blocks_in + lag_blocks - 3
    t = lax.axis_index("tm")
    e = lax.axis_index("pairs")
    core, x, y = lax.rem(e, 2), lax.rem(e // 2, 2), e // 4
    ex, ey, ec = e + 2 - 4 * x, e + 4 - 8 * y, e + 1 - 2 * core
    ed = ex + 4 - 8 * y
    cx, cy, cd = ex + 1 - 2 * core, ey + 1 - 2 * core, ed + 1 - 2 * core

    near, far = t + 1 - 2 * lax.rem(t, 2), 3 - t
    inner = (t == 1) | (t == 2)

    load_asked = pltpu.make_async_copy(asked_hbm, asked_ref, local.at[0])
    load_record = pltpu.make_async_copy(record_hbm, record_ref, local.at[1])
    load_record.start()
    load_asked.start()
    barrier = pltpu.get_barrier_semaphore()
    for peer in ((t, ex), (t, ey), (t, ec), (near, e), (far, e)):
        pl.semaphore_signal(barrier, inc=1, device_id=peer, device_id_type=MESH)

    row_index = lax.broadcasted_iota(jnp.int32, (HALF, HALF), 0)
    lane_index = lax.broadcasted_iota(jnp.int32, (HALF, HALF), 1)
    mirror = jnp.where(row_index + lane_index == HALF - 1, 1.0, 0.0).astype(jnp.bfloat16)

    def flip_halves(tile):
        return jnp.dot(tile, mirror, preferred_element_type=jnp.float32)

    stations = traces // comps
    load_record.wait()
    for comp in range(comps):
        values = record_ref[comp].astype(jnp.float32)
        values = values - jnp.mean(values, axis=-1, keepdims=True)
        power_mean = jnp.mean(values * values, axis=-1, keepdims=True)
        values = values * lax.rsqrt(power_mean + 1e-06)
        for m in range(blocks_in):
            rows = pl.ds(comp * blocks_in + m, stations, stride=comps * blocks_in)
            for h in (0, 1):
                lane = m * BLOCK + h * HALF
                rows32[h, rows, :] = values[:, lane : lane + HALF]
    for h in (0, 1):
        blks[0][e, :, :, h * HALF : (h + 1) * HALF] = (
            flip_halves(rows32[h].astype(jnp.bfloat16))
            .astype(jnp.bfloat16)
            .reshape(traces, blocks_in, HALF)
        )
    pl.semaphore_wait(barrier, 5)

    def plane_copy(k, kind, origin, target):
        blk = blks[k]
        if kind == DIAG_A:
            ref = blk.at[origin, pl.ds(0, traces // 2)]
        elif kind == DIAG_B:
            ref = blk.at[origin, pl.ds(traces // 2, traces // 2)]
        else:
            ref = blk.at[origin]
        return pltpu.make_async_remote_copy(
            src_ref=ref, dst_ref=ref,
            send_sem=send.at[k, kind], recv_sem=recv.at[k, kind],
            device_id=(t, target), device_id_type=MESH,
        )

    def z_copy(index, source, slot, target):
        return pltpu.make_async_remote_copy(
            src_ref=blks[source].at[e], dst_ref=blks[slot].at[e],
            send_sem=zsend.at[index], recv_sem=zrecv.at[slot - 1],
            device_id=(target, e), device_id_type=MESH,
        )

    own_near = z_copy(0, 0, 1, near)
    own_far = z_copy(1, 0, 2, far)
    near_to_far = z_copy(2, 1, 3, far)
    far_to_near = z_copy(3, 2, 2, near)
    rest_to_near = z_copy(4, 3, 3, near)

    def wait_window(k):
        z_copy(0, 0, k, near).wait_recv()

    def send_own(k):
        plane_copy(k, FROM_X, e, ex).start()
        plane_copy(k, FROM_Y, e, ey).start()
        plane_copy(k, CORE_OWN, e, ec).start()

    def forward_xy(k):
        plane_copy(k, FROM_X, ex, ex).wait_recv()
        plane_copy(k, DIAG_A, ex, ey).start()
        plane_copy(k, CORE_X, ex, ec).start()
        plane_copy(k, FROM_Y, ey, ey).wait_recv()
        plane_copy(k, DIAG_B, ey, ex).start()
        plane_copy(k, CORE_Y, ey, ec).start()

    def forward_diag(k):
        plane_copy(k, DIAG_A, ed, ey).wait_recv()
        plane_copy(k, DIAG_B, ed, ex).wait_recv()
        plane_copy(k, CORE_D, ed, ec).start()

    def wait_core(k):
        plane_copy(k, CORE_OWN, ec, ec).wait_recv()
        plane_copy(k, CORE_X, cx, ec).wait_recv()
        plane_copy(k, CORE_Y, cy, ec).wait_recv()
        plane_copy(k, CORE_D, cd, ec).wait_recv()

    below = lane_index <= row_index
    nothing = jnp.zeros((HALF, HALF), jnp.bfloat16)
    first_chunk = 2 * first_s

    def put(k, j, chunk, tile):
        lane = (chunk - first_chunk) * HALF
        hankel[own_count * k + j, :, lane : lane + HALF] = tile

    def build(k):
        def one(j, carry):
            for h in (0, 1):
                lanes = slice(h * HALF, (h + 1) * HALF)
                own32[:, lanes] = flip_halves(blks[k][e, own_count * t + j, :, lanes])
            before = nothing
            for c in range(2 * blocks_in + 1):
                if c < 2 * blocks_in:
                    half = c % 2
                    row = own32[c // 2 : c // 2 + 1, half * HALF : (half + 1) * HALF]
                    skewed = pltpu.roll(
                        jnp.broadcast_to(row, (16, HALF)), 1, 1, stride=1, stride_axis=0
                    ).astype(jnp.bfloat16)
                    now = jnp.concatenate(
                        [skewed] + [pltpu.roll(skewed, 16 * a, 1) for a in range(1, HALF // 16)], axis=0
                    )
                else:
                    now = nothing
                put(k, j, c + lag_blocks - 1, jnp.where(below, before, now))
                before = now
            return carry

        lax.fori_loop(0, own_count, one, 0)

    def correlate_window(k, between=lambda: None):
        blk = blks[k]
        for d in range(owners):
            for i in range(capacity):
                station = asked_ref[e, i, d]
                slot = (d * capacity + i) * comps * blocks_in
                station_rows = (
                    blk[d, pl.ds(station * comps, comps)]
                    .astype(jnp.float32)
                    .reshape(comps * blocks_in, BLOCK)
                )
                for h in (0, 1):
                    pool32[h, slot : slot + comps * blocks_in, :] = station_rows[
                        :, h * HALF : (h + 1) * HALF
                    ]
        for m in range(blocks_in):
            for h in (0, 1):
                part = pool32[h, pl.ds(m, pool, stride=blocks_in), :].astype(jnp.bfloat16)
                pool16[m, :, h * HALF : (h + 1) * HALF] = part

        def one(j, carry):
            empty = jnp.zeros((pool, BLOCK), jnp.bfloat16)
            left = jnp.concatenate(
                [
                    jnp.concatenate(
                        [
                            pool16[s - q] if 0 <= s - q < blocks_in else empty
                            for s in range(first_s, last_s + 1)
                        ],
                        axis=1,
                    )
                    for q in reversed(range(lag_blocks))
                ],
                axis=0,
            )
            index = own_count * k + j
            right = jnp.concatenate(
                [
                    hankel[index, :, lane : lane + BLOCK]
                    for s in range(first_s, last_s + 1)
                    for lane in ((2 * s - first_chunk) * HALF, (2 * s + 1 - first_chunk) * HALF)
                ],
                axis=0,
            )
            term = jnp.dot(left, right, preferred_element_type=jnp.float32)
            if k == 0:
                cc_ref[j] = term
            else:
                cc_ref[j] += term
            return carry

        lax.fori_loop(0, own_count - 1, one, 0)
        between()
        one(own_count - 1, 0)

    own_near.start()

    @pl.when(inner)
    def _():
        own_far.start()

    send_own(0)
    for k in range(4):
        for j in range(own_count):
            put(k, j, first_chunk, nothing)
            put(k, j, 2 * last_s + 2, nothing)

    build(0)
    wait_window(1)

    @pl.when(inner)
    def _():
        near_to_far.start()
        wait_window(2)
        far_to_near.start()

    send_own(1)
    forward_xy(0)
    build(1)
    forward_diag(0)

    @pl.when(jnp.logical_not(inner))
    def _():
        wait_window(2)

    @pl.when(inner)
    def _():
        wait_window(3)
        rest_to_near.start()

    send_own(2)
    forward_xy(1)
    load_asked.wait()
    wait_core(0)
    correlate_window(0)
    forward_diag(1)
    build(2)

    @pl.when(jnp.logical_not(inner))
    def _():
        wait_window(3)

    send_own(3)
    forward_xy(2)
    wait_core(1)
    correlate_window(1)
    forward_diag(2)
    build(3)
    forward_xy(3)
    wait_core(2)
    correlate_window(2, functools.partial(forward_diag, 3))
    wait_core(3)
    correlate_window(3)

    own_near.wait_send()

    @pl.when(inner)
    def _():
        own_far.wait_send()
        near_to_far.wait_send()
        far_to_near.wait_send()
        rest_to_near.wait_send()

    for k in range(4):
        plane_copy(k, FROM_X, e, ex).wait_send()
        plane_copy(k, FROM_Y, e, ey).wait_send()
        plane_copy(k, CORE_OWN, e, ec).wait_send()
        plane_copy(k, DIAG_A, ex, ey).wait_send()
        plane_copy(k, CORE_X, ex, ec).wait_send()
        plane_copy(k, DIAG_B, ey, ex).wait_send()
        plane_copy(k, CORE_Y, ey, ec).wait_send()
        plane_copy(k, CORE_D, ed, ec).wait_send()


def select_kernel(scale, own_count, comps, lag_blocks, counts_ref, partners_ref, codes_ref, cc_ref, out_ref):
    t = lax.axis_index("tm")
    pool = cc_ref.shape[1] // lag_blocks
    slots = partners_ref.shape[2]
    pool_row = lax.broadcasted_iota(jnp.int32, (pool, slots), 0)
    slot_lane = lax.broadcasted_iota(jnp.int32, (pool, slots), 1)
    dims = (((0,), (0,)), ((), ()))
    for j in range(own_count):
        trace = own_count * t + j
        wanted = partners_ref[trace] * comps + codes_ref[trace]
        hit = (wanted == pool_row) & (slot_lane < counts_ref[0, trace])
        chosen = jnp.where(hit, 1.0, 0.0).astype(jnp.bfloat16)
        for q in range(lag_blocks):
            part = cc_ref[j, q * pool : (q + 1) * pool, :]
            high = part.astype(jnp.bfloat16)
            rest = part - high.astype(jnp.float32)
            middle = rest.astype(jnp.bfloat16)
            low = (rest - middle.astype(jnp.float32)).astype(jnp.bfloat16)
            total = lax.dot_general(chosen, low, dims, preferred_element_type=jnp.float32)
            total += lax.dot_general(chosen, middle, dims, preferred_element_type=jnp.float32)
            total += lax.dot_general(chosen, high, dims, preferred_element_type=jnp.float32)
            lag = (lag_blocks - 1 - q) * BLOCK
            out_ref[0, j * slots : (j + 1) * slots, lag : lag + BLOCK] = total * scale


def gathered_shards(record, requested, partners, codes, counts):
    stations, comps, _, window_len = record.shape
    owners, capacity = requested.shape[1:]
    traces = stations * comps
    windows = lax.axis_size("tm")
    own_count = traces // windows
    blocks_in, lag_blocks = window_len // BLOCK, LAGS // BLOCK
    pool = owners * capacity * comps
    depth = (blocks_in + lag_blocks - 3) * BLOCK
    slots = partners.shape[2]
    cc_shape = jax.ShapeDtypeStruct((own_count, lag_blocks * pool, BLOCK), jnp.float32)
    dims = (traces, blocks_in, owners, capacity, comps, own_count, lag_blocks)
    vmem = pl.BlockSpec(memory_space=pltpu.VMEM)
    smem = pl.BlockSpec(memory_space=pltpu.SMEM)
    cc = pl.pallas_call(
        functools.partial(exchange_kernel, dims),
        out_shape=cc_shape,
        in_specs=[pl.BlockSpec(memory_space=pltpu.HBM)] * 2,
        out_specs=vmem,
        scratch_shapes=[pltpu.VMEM((owners, traces, blocks_in, BLOCK), jnp.bfloat16)] * 4
        + [
            pltpu.SMEM((owners, capacity, owners), jnp.int32),
            pltpu.VMEM((comps, stations, window_len), jnp.bfloat16),
            pltpu.VMEM((2, traces * blocks_in, HALF), jnp.float32),
            pltpu.VMEM((2, pool * blocks_in, HALF), jnp.float32),
            pltpu.VMEM((blocks_in, BLOCK), jnp.float32),
            pltpu.VMEM((blocks_in, pool, BLOCK), jnp.bfloat16),
            pltpu.VMEM((4 * own_count, HALF, depth + HALF), jnp.bfloat16),
            pltpu.SemaphoreType.DMA((4, 8)),
            pltpu.SemaphoreType.DMA((4, 8)),
            pltpu.SemaphoreType.DMA((5,)),
            pltpu.SemaphoreType.DMA((3,)),
            pltpu.SemaphoreType.DMA((2,)),
        ],
        compiler_params=pltpu.CompilerParams(
            collective_id=0, has_side_effects=True, vmem_limit_bytes=60 * 1024 * 1024
        ),
    )(requested.transpose(0, 2, 1), record.transpose(2, 1, 0, 3)[0])
    return pl.pallas_call(
        functools.partial(
            select_kernel, 1.0 / math.sqrt(window_len * windows), own_count, comps, lag_blocks
        ),
        out_shape=jax.ShapeDtypeStruct((1, own_count * slots, LAGS), jnp.float32),
        in_specs=[smem, vmem, vmem, vmem],
        out_specs=vmem,
        compiler_params=pltpu.CompilerParams(vmem_limit_bytes=16 * 1024 * 1024),
    )(counts, partners.transpose(1, 0, 2), codes.transpose(1, 0, 2), cc)


def solution(mesh):
    def body(record, requested, partners, codes, counts):
        planes = lax.axis_size("tm") == 4 and lax.axis_size("pairs") == 8
        stations, comps, window_count, window_len = record.shape
        fits = (
            window_count == 1
            and stations == 4
            and window_len % BLOCK == 0
            and LAGS == 4 * BLOCK
        )
        form = gathered_shards if planes and fits else shards
        return form(record, requested, partners, codes, counts)

    return jax.shard_map(
        body,
        mesh=mesh,
        in_specs=(
            P("pairs", None, "tm", None),
            P(),
            P("pairs", None, None),
            P("pairs", None, None),
            P("pairs", None),
        ),
        out_specs=P("pairs", "tm", None),
        check_vma=False,
    )
```

```python
import functools
import math

import jax
import jax.numpy as jnp
from jax import lax
from jax.experimental import pallas as pl
from jax.experimental.pallas import tpu as pltpu
from jax.sharding import PartitionSpec as P

LAGS = 1024


def normalize(traces):
    values = traces.astype(jnp.float32)
    values = values - jnp.mean(values, axis=-1, keepdims=True)
    power_mean = jnp.mean(values * values, axis=-1, keepdims=True)
    return (values * lax.rsqrt(power_mean + 1e-06)).astype(jnp.bfloat16)


def correlate(own_trace, partner_rows, lag_count, block_len):
    window_len = own_trace.shape[0]
    half_lag = lag_count // 2
    padded = jnp.pad(own_trace, (half_lag, half_lag + block_len))
    length = padded.shape[0]
    spread = jnp.broadcast_to(padded, (block_len, length)).reshape(-1)
    spread = jnp.pad(spread, (0, block_len))
    skewed = spread.reshape(block_len, length + 1)[:, : window_len + lag_count]
    hankel = skewed.reshape(block_len, (window_len + lag_count) // block_len, block_len)
    blocks_in = window_len // block_len
    pieces = partner_rows.reshape(partner_rows.shape[0], blocks_in, block_len)
    outputs = []
    for offset in range(lag_count // block_len):
        window_view = hankel[:, offset : offset + blocks_in, :]
        outputs.append(
            jnp.einsum("pmi,imr->pr", pieces, window_view, preferred_element_type=jnp.float32)
        )
    return jnp.concatenate(outputs, axis=1)


def shards(record, requested, partners, codes, counts):
    whitened = normalize(record)
    local_stations, comp_count, window_count, window_len = whitened.shape
    owners = lax.axis_size("pairs")
    capacity = requested.shape[2]
    per_trace = partners.shape[2]
    trace_count = local_stations * comp_count
    block_len = math.gcd(math.gcd(128, window_len), LAGS)
    own_index = lax.axis_index("pairs")
    slot_ids = partners[0]
    comp_ids = codes[0]
    everyone = lax.all_gather(whitened, "pairs", axis=0, tiled=True)
    trace_pool = everyone.reshape(owners * local_stations * comp_count, window_count, window_len)
    asked_table = lax.dynamic_index_in_dim(requested, own_index, axis=0, keepdims=False)
    station_of = (
        asked_table + jnp.arange(owners, dtype=jnp.int32)[:, None] * local_stations
    ).reshape(-1)
    matches = slot_ids[:, :, None] == jnp.arange(owners * capacity, dtype=jnp.int32)[None, None, :]
    stations = jnp.sum(jnp.where(matches, station_of[None, None, :], 0), axis=-1)
    row_ids = stations * comp_count + comp_ids
    picked = jnp.take(trace_pool, row_ids.reshape(-1), axis=0)
    live_rows = jnp.arange(per_trace, dtype=jnp.int32)[None, :] < counts[0][:, None]
    picked = jnp.where(live_rows.reshape(-1)[:, None, None], picked, jnp.zeros((), jnp.bfloat16))
    picked = picked.reshape(trace_count, per_trace, window_count, window_len)
    picked = jnp.moveaxis(picked, 2, 1).reshape(trace_count * window_count, per_trace, window_len)
    own_rows = whitened.reshape(trace_count * window_count, window_len)

    def one_trace(operands):
        own_row, partner_rows = operands
        return correlate(own_row, partner_rows, LAGS, block_len)

    lagged = lax.map(one_trace, (own_rows, picked))
    lagged = lagged.reshape(trace_count, window_count, per_trace, LAGS)
    total_windows = window_count * lax.axis_size("tm")
    window_term = jnp.sum(lagged, axis=1) * (1.0 / math.sqrt(window_len * total_windows))
    window_term = window_term.reshape(1, trace_count * per_trace, LAGS)
    return lax.psum_scatter(window_term, "tm", scatter_dimension=1, tiled=True)


MESH = pl.DeviceIdType.MESH
HALF = 128
BLOCK = 2 * HALF
FROM_X, FROM_Y, DIAG_A, DIAG_B, CORE_OWN, CORE_X, CORE_Y, CORE_D = range(8)


def exchange_kernel(
    dims, asked_hbm, record_hbm, cc_ref, *scratch
):
    traces, blocks_in, owners, capacity, comps, own_count, lag_blocks = dims
    blks = scratch[:4]
    (asked_ref, record_ref, rows32, pool32, own32, pool16, hankel) = scratch[4:11]
    (send, recv, zsend, zrecv, local) = scratch[11:]
    pool = owners * capacity * comps
    first_s, last_s = 1, blocks_in + lag_blocks - 3
    t = lax.axis_index("tm")
    e = lax.axis_index("pairs")
    core, x, y = lax.rem(e, 2), lax.rem(e // 2, 2), e // 4
    ex, ey, ec = e + 2 - 4 * x, e + 4 - 8 * y, e + 1 - 2 * core
    ed = ex + 4 - 8 * y
    cx, cy, cd = ex + 1 - 2 * core, ey + 1 - 2 * core, ed + 1 - 2 * core

    near, far = t + 1 - 2 * lax.rem(t, 2), 3 - t
    inner = (t == 1) | (t == 2)

    load_asked = pltpu.make_async_copy(asked_hbm, asked_ref, local.at[0])
    load_record = pltpu.make_async_copy(record_hbm, record_ref, local.at[1])
    load_record.start()
    load_asked.start()
    barrier = pltpu.get_barrier_semaphore()
    for peer in ((t, ex), (t, ey), (t, ec), (near, e), (far, e)):
        pl.semaphore_signal(barrier, inc=1, device_id=peer, device_id_type=MESH)

    row_index = lax.broadcasted_iota(jnp.int32, (HALF, HALF), 0)
    lane_index = lax.broadcasted_iota(jnp.int32, (HALF, HALF), 1)
    mirror = jnp.where(row_index + lane_index == HALF - 1, 1.0, 0.0).astype(jnp.bfloat16)

    def flip_halves(tile):
        return jnp.dot(tile, mirror, preferred_element_type=jnp.float32)

    stations = traces // comps
    load_record.wait()

    def whiten(comp, carry):
        values = record_ref[comp].astype(jnp.float32)
        values = values - jnp.mean(values, axis=-1, keepdims=True)
        power_mean = jnp.mean(values * values, axis=-1, keepdims=True)
        values = values * lax.rsqrt(power_mean + 1e-06)
        for m in range(blocks_in):
            rows = pl.ds(comp * blocks_in + m, stations, stride=comps * blocks_in)
            for h in (0, 1):
                lane = m * BLOCK + h * HALF
                rows32[h, rows, :] = values[:, lane : lane + HALF]
        return carry

    lax.fori_loop(0, comps, whiten, 0)
    for h in (0, 1):
        blks[0][e, :, :, h * HALF : (h + 1) * HALF] = (
            flip_halves(rows32[h].astype(jnp.bfloat16))
            .astype(jnp.bfloat16)
            .reshape(traces, blocks_in, HALF)
        )
    pl.semaphore_wait(barrier, 5)

    def plane_copy(k, kind, origin, target):
        blk = blks[k]
        if kind == DIAG_A:
            ref = blk.at[origin, pl.ds(0, traces // 2)]
        elif kind == DIAG_B:
            ref = blk.at[origin, pl.ds(traces // 2, traces // 2)]
        else:
            ref = blk.at[origin]
        return pltpu.make_async_remote_copy(
            src_ref=ref, dst_ref=ref,
            send_sem=send.at[k, kind], recv_sem=recv.at[k, kind],
            device_id=(t, target), device_id_type=MESH,
        )

    def z_copy(index, source, slot, target):
        return pltpu.make_async_remote_copy(
            src_ref=blks[source].at[e], dst_ref=blks[slot].at[e],
            send_sem=zsend.at[index], recv_sem=zrecv.at[slot - 1],
            device_id=(target, e), device_id_type=MESH,
        )

    own_near = z_copy(0, 0, 1, near)
    own_far = z_copy(1, 0, 2, far)
    near_to_far = z_copy(2, 1, 3, far)
    far_to_near = z_copy(3, 2, 2, near)
    rest_to_near = z_copy(4, 3, 3, near)

    def wait_window(k):
        z_copy(0, 0, k, near).wait_recv()

    def send_own(k):
        plane_copy(k, FROM_X, e, ex).start()
        plane_copy(k, FROM_Y, e, ey).start()
        plane_copy(k, CORE_OWN, e, ec).start()

    def forward_xy(k):
        plane_copy(k, FROM_X, ex, ex).wait_recv()
        plane_copy(k, DIAG_A, ex, ey).start()
        plane_copy(k, CORE_X, ex, ec).start()
        plane_copy(k, FROM_Y, ey, ey).wait_recv()
        plane_copy(k, DIAG_B, ey, ex).start()
        plane_copy(k, CORE_Y, ey, ec).start()

    def forward_diag(k):
        plane_copy(k, DIAG_A, ed, ey).wait_recv()
        plane_copy(k, DIAG_B, ed, ex).wait_recv()
        plane_copy(k, CORE_D, ed, ec).start()

    def wait_core(k):
        plane_copy(k, CORE_OWN, ec, ec).wait_recv()
        plane_copy(k, CORE_X, cx, ec).wait_recv()
        plane_copy(k, CORE_Y, cy, ec).wait_recv()
        plane_copy(k, CORE_D, cd, ec).wait_recv()

    below = lane_index <= row_index
    nothing = jnp.zeros((HALF, HALF), jnp.bfloat16)
    first_chunk = 2 * first_s

    last_chunk = 2 * last_s + 2

    def unmirror(k):
        for j in range(own_count):
            for h in (0, 1):
                lanes = slice(h * HALF, (h + 1) * HALF)
                own32[j, :, lanes] = flip_halves(blks[k][e, own_count * t + j, :, lanes])

    def build(n):
        def one(j, carry):
            index = own_count * n + j

            def eight_blocks(g, before):
                rows = own32[j, pl.ds(pl.multiple_of(8 * g, 8), 8), :]
                for b in range(8):
                    m = 8 * g + b
                    for half in (0, 1):
                        row = rows[b : b + 1, half * HALF : (half + 1) * HALF]
                        skewed = pltpu.roll(
                            jnp.broadcast_to(row, (16, HALF)), 1, 1, stride=1, stride_axis=0
                        ).astype(jnp.bfloat16)
                        now = jnp.concatenate(
                            [skewed] + [pltpu.roll(skewed, 16 * a, 1) for a in range(1, HALF // 16)],
                            axis=0,
                        )
                        lane = (2 * m + half + lag_blocks - 1 - first_chunk) * HALF
                        hankel[index, :, pl.ds(pl.multiple_of(lane, HALF), HALF)] = jnp.where(
                            below, before, now
                        )
                        before = now
                return before

            before = lax.fori_loop(0, blocks_in // 8, eight_blocks, nothing)
            lane = (2 * blocks_in + lag_blocks - 1 - first_chunk) * HALF
            hankel[index, :, lane : lane + HALF] = jnp.where(below, before, nothing)
            hankel[index, :, :HALF] = nothing
            lane = (last_chunk - first_chunk) * HALF
            hankel[index, :, lane : lane + HALF] = nothing
            return carry

        lax.fori_loop(0, own_count, one, 0)

    def pick(k):
        blk = blks[k]

        def one(slot, carry):
            d, i = slot // capacity, lax.rem(slot, capacity)
            station = asked_ref[e, i, d]
            rows = (
                blk[d, pl.ds(station * comps, comps)]
                .astype(jnp.float32)
                .reshape(comps * blocks_in, BLOCK)
            )
            start = pl.multiple_of(slot * (comps * blocks_in), comps * blocks_in)
            for h in (0, 1):
                pool32[h, pl.ds(start, comps * blocks_in), :] = rows[:, h * HALF : (h + 1) * HALF]
            return carry

        lax.fori_loop(0, owners * capacity, one, 0)

    def correlate(n):
        for m in range(blocks_in):
            for h in (0, 1):
                part = pool32[h, pl.ds(m, pool, stride=blocks_in), :].astype(jnp.bfloat16)
                pool16[m, :, h * HALF : (h + 1) * HALF] = part

        def one(j, carry):
            empty = jnp.zeros((pool, BLOCK), jnp.bfloat16)
            left = jnp.concatenate(
                [
                    jnp.concatenate(
                        [
                            pool16[s - q] if 0 <= s - q < blocks_in else empty
                            for s in range(first_s, last_s + 1)
                        ],
                        axis=1,
                    )
                    for q in reversed(range(lag_blocks))
                ],
                axis=0,
            )
            index = own_count * n + j
            right = jnp.concatenate(
                [
                    hankel[index, :, lane : lane + BLOCK]
                    for s in range(first_s, last_s + 1)
                    for lane in ((2 * s - first_chunk) * HALF, (2 * s + 1 - first_chunk) * HALF)
                ],
                axis=0,
            )
            term = jnp.dot(left, right, preferred_element_type=jnp.float32)

            @pl.when(n == 0)
            def _():
                cc_ref[j] = term

            @pl.when(n > 0)
            def _():
                cc_ref[j] += term

            @pl.when((n == 2) & (j == own_count - 2))
            def _():
                forward_diag(3)

            return carry

        lax.fori_loop(0, own_count, one, 0)

    own_near.start()

    @pl.when(inner)
    def _():
        own_far.start()

    send_own(0)
    def before_build(n):
        if n == 1:
            wait_window(1)

            @pl.when(inner)
            def _():
                near_to_far.start()
                wait_window(2)
                far_to_near.start()

            send_own(1)
            forward_xy(0)
        if n == 2:
            forward_diag(0)

            @pl.when(jnp.logical_not(inner))
            def _():
                wait_window(2)

            @pl.when(inner)
            def _():
                wait_window(3)
                rest_to_near.start()

            send_own(2)
            forward_xy(1)
            load_asked.wait()
        if n == 3:
            forward_diag(1)

            @pl.when(jnp.logical_not(inner))
            def _():
                wait_window(3)

            send_own(3)
            forward_xy(2)
        if n == 4:
            forward_diag(2)
            forward_xy(3)
        if n < 4:
            unmirror(n)

    def before_correlate(n):
        wait_core(n)
        pick(n)

    def step(n, carry):
        for k in range(5):
            pl.when(n == k)(functools.partial(before_build, k))
        pl.when(n < 4)(functools.partial(build, n))
        for k in range(4):
            pl.when(n == k + 2)(functools.partial(before_correlate, k))
        pl.when(n >= 2)(functools.partial(correlate, n - 2))
        return carry

    lax.fori_loop(0, 6, step, 0)

    own_near.wait_send()

    @pl.when(inner)
    def _():
        own_far.wait_send()
        near_to_far.wait_send()
        far_to_near.wait_send()
        rest_to_near.wait_send()

    for k in range(4):
        plane_copy(k, FROM_X, e, ex).wait_send()
        plane_copy(k, FROM_Y, e, ey).wait_send()
        plane_copy(k, CORE_OWN, e, ec).wait_send()
        plane_copy(k, DIAG_A, ex, ey).wait_send()
        plane_copy(k, CORE_X, ex, ec).wait_send()
        plane_copy(k, DIAG_B, ey, ex).wait_send()
        plane_copy(k, CORE_Y, ey, ec).wait_send()
        plane_copy(k, CORE_D, ed, ec).wait_send()


def select_kernel(scale, own_count, comps, lag_blocks, counts_ref, partners_ref, codes_ref, cc_ref, out_ref):
    trace = own_count * lax.axis_index("tm") + pl.program_id(0)
    pool = cc_ref.shape[1] // lag_blocks
    slots = partners_ref.shape[2]
    pool_row = lax.broadcasted_iota(jnp.int32, (pool, slots), 0)
    slot_lane = lax.broadcasted_iota(jnp.int32, (pool, slots), 1)
    dims = (((0,), (0,)), ((), ()))
    wanted = partners_ref[trace] * comps + codes_ref[trace]
    hit = (wanted == pool_row) & (slot_lane < counts_ref[0, trace])
    chosen = jnp.where(hit, 1.0, 0.0).astype(jnp.bfloat16)
    for q in range(lag_blocks):
        part = cc_ref[0, q * pool : (q + 1) * pool, :]
        high = part.astype(jnp.bfloat16)
        low = (part - high.astype(jnp.float32)).astype(jnp.bfloat16)
        total = lax.dot_general(chosen, low, dims, preferred_element_type=jnp.float32)
        total += lax.dot_general(chosen, high, dims, preferred_element_type=jnp.float32)
        lag = (lag_blocks - 1 - q) * BLOCK
        out_ref[0, :, lag : lag + BLOCK] = total * scale


def gathered_shards(record, requested, partners, codes, counts):
    stations, comps, _, window_len = record.shape
    owners, capacity = requested.shape[1:]
    traces = stations * comps
    windows = lax.axis_size("tm")
    own_count = traces // windows
    blocks_in, lag_blocks = window_len // BLOCK, LAGS // BLOCK
    pool = owners * capacity * comps
    depth = (blocks_in + lag_blocks - 3) * BLOCK
    slots = partners.shape[2]
    cc_shape = jax.ShapeDtypeStruct((own_count, lag_blocks * pool, BLOCK), jnp.float32)
    dims = (traces, blocks_in, owners, capacity, comps, own_count, lag_blocks)
    vmem = pl.BlockSpec(memory_space=pltpu.VMEM)
    smem = pl.BlockSpec(memory_space=pltpu.SMEM)
    cc = pl.pallas_call(
        functools.partial(exchange_kernel, dims),
        out_shape=cc_shape,
        in_specs=[pl.BlockSpec(memory_space=pltpu.HBM)] * 2,
        out_specs=vmem,
        scratch_shapes=[pltpu.VMEM((owners, traces, blocks_in, BLOCK), jnp.bfloat16)] * 4
        + [
            pltpu.SMEM((owners, capacity, owners), jnp.int32),
            pltpu.VMEM((comps, stations, window_len), jnp.bfloat16),
            pltpu.VMEM((2, traces * blocks_in, HALF), jnp.float32),
            pltpu.VMEM((2, pool * blocks_in, HALF), jnp.float32),
            pltpu.VMEM((own_count, blocks_in, BLOCK), jnp.float32),
            pltpu.VMEM((blocks_in, pool, BLOCK), jnp.bfloat16),
            pltpu.VMEM((4 * own_count, HALF, depth + HALF), jnp.bfloat16),
            pltpu.SemaphoreType.DMA((4, 8)),
            pltpu.SemaphoreType.DMA((4, 8)),
            pltpu.SemaphoreType.DMA((5,)),
            pltpu.SemaphoreType.DMA((3,)),
            pltpu.SemaphoreType.DMA((2,)),
        ],
        compiler_params=pltpu.CompilerParams(
            collective_id=0, has_side_effects=True, vmem_limit_bytes=60 * 1024 * 1024
        ),
    )(requested.transpose(0, 2, 1), record.transpose(2, 1, 0, 3)[0])
    return pl.pallas_call(
        functools.partial(
            select_kernel, 1.0 / math.sqrt(window_len * windows), own_count, comps, lag_blocks
        ),
        out_shape=jax.ShapeDtypeStruct((1, own_count * slots, LAGS), jnp.float32),
        grid=(own_count,),
        in_specs=[smem, vmem, vmem, pl.BlockSpec((1, lag_blocks * pool, BLOCK), lambda j: (j, 0, 0))],
        out_specs=pl.BlockSpec((1, slots, LAGS), lambda j: (0, j, 0)),
        compiler_params=pltpu.CompilerParams(vmem_limit_bytes=60 * 1024 * 1024),
    )(counts, partners.transpose(1, 0, 2), codes.transpose(1, 0, 2), cc)


def solution(mesh):
    def body(record, requested, partners, codes, counts):
        planes = lax.axis_size("tm") == 4 and lax.axis_size("pairs") == 8
        stations, comps, window_count, window_len = record.shape
        fits = (
            window_count == 1
            and stations == 4
            and window_len % (8 * BLOCK) == 0
            and LAGS == 4 * BLOCK
        )
        form = gathered_shards if planes and fits else shards
        return form(record, requested, partners, codes, counts)

    return jax.shard_map(
        body,
        mesh=mesh,
        in_specs=(
            P("pairs", None, "tm", None),
            P(),
            P("pairs", None, None),
            P("pairs", None, None),
            P("pairs", None),
        ),
        out_specs=P("pairs", "tm", None),
        check_vma=False,
    )
```

```python
import functools
import math

import jax
import jax.numpy as jnp
from jax import lax
from jax.experimental import pallas as pl
from jax.experimental.pallas import tpu as pltpu
from jax.sharding import PartitionSpec as P

LAGS = 1024


def normalize(traces):
    values = traces.astype(jnp.float32)
    values = values - jnp.mean(values, axis=-1, keepdims=True)
    power_mean = jnp.mean(values * values, axis=-1, keepdims=True)
    return (values * lax.rsqrt(power_mean + 1e-06)).astype(jnp.bfloat16)


def correlate(own_trace, partner_rows, lag_count, block_len):
    window_len = own_trace.shape[0]
    half_lag = lag_count // 2
    padded = jnp.pad(own_trace, (half_lag, half_lag + block_len))
    length = padded.shape[0]
    spread = jnp.broadcast_to(padded, (block_len, length)).reshape(-1)
    spread = jnp.pad(spread, (0, block_len))
    skewed = spread.reshape(block_len, length + 1)[:, : window_len + lag_count]
    hankel = skewed.reshape(block_len, (window_len + lag_count) // block_len, block_len)
    blocks_in = window_len // block_len
    pieces = partner_rows.reshape(partner_rows.shape[0], blocks_in, block_len)
    outputs = []
    for offset in range(lag_count // block_len):
        window_view = hankel[:, offset : offset + blocks_in, :]
        outputs.append(
            jnp.einsum("pmi,imr->pr", pieces, window_view, preferred_element_type=jnp.float32)
        )
    return jnp.concatenate(outputs, axis=1)


def shards(record, requested, partners, codes, counts):
    whitened = normalize(record)
    local_stations, comp_count, window_count, window_len = whitened.shape
    owners = lax.axis_size("pairs")
    capacity = requested.shape[2]
    per_trace = partners.shape[2]
    trace_count = local_stations * comp_count
    block_len = math.gcd(math.gcd(128, window_len), LAGS)
    own_index = lax.axis_index("pairs")
    slot_ids = partners[0]
    comp_ids = codes[0]
    everyone = lax.all_gather(whitened, "pairs", axis=0, tiled=True)
    trace_pool = everyone.reshape(owners * local_stations * comp_count, window_count, window_len)
    asked_table = lax.dynamic_index_in_dim(requested, own_index, axis=0, keepdims=False)
    station_of = (
        asked_table + jnp.arange(owners, dtype=jnp.int32)[:, None] * local_stations
    ).reshape(-1)
    matches = slot_ids[:, :, None] == jnp.arange(owners * capacity, dtype=jnp.int32)[None, None, :]
    stations = jnp.sum(jnp.where(matches, station_of[None, None, :], 0), axis=-1)
    row_ids = stations * comp_count + comp_ids
    picked = jnp.take(trace_pool, row_ids.reshape(-1), axis=0)
    live_rows = jnp.arange(per_trace, dtype=jnp.int32)[None, :] < counts[0][:, None]
    picked = jnp.where(live_rows.reshape(-1)[:, None, None], picked, jnp.zeros((), jnp.bfloat16))
    picked = picked.reshape(trace_count, per_trace, window_count, window_len)
    picked = jnp.moveaxis(picked, 2, 1).reshape(trace_count * window_count, per_trace, window_len)
    own_rows = whitened.reshape(trace_count * window_count, window_len)

    def one_trace(operands):
        own_row, partner_rows = operands
        return correlate(own_row, partner_rows, LAGS, block_len)

    lagged = lax.map(one_trace, (own_rows, picked))
    lagged = lagged.reshape(trace_count, window_count, per_trace, LAGS)
    total_windows = window_count * lax.axis_size("tm")
    window_term = jnp.sum(lagged, axis=1) * (1.0 / math.sqrt(window_len * total_windows))
    window_term = window_term.reshape(1, trace_count * per_trace, LAGS)
    return lax.psum_scatter(window_term, "tm", scatter_dimension=1, tiled=True)


MESH = pl.DeviceIdType.MESH
HALF = 128
BLOCK = 2 * HALF
FROM_X, FROM_Y, DIAG_A, DIAG_B, CORE_OWN, CORE_X, CORE_Y, CORE_D = range(8)


def exchange_kernel(
    dims, asked_hbm, record_hbm, cc_ref, *scratch
):
    traces, blocks_in, owners, capacity, comps, own_count, lag_blocks = dims
    blks = scratch[:4]
    (asked_ref, record_ref, rows32, pool32, own32, pool16, hankel) = scratch[4:11]
    (send, recv, zsend, zrecv, local) = scratch[11:]
    pool = owners * capacity * comps
    first_s, last_s = 1, blocks_in + lag_blocks - 3
    t = lax.axis_index("tm")
    e = lax.axis_index("pairs")
    core, x, y = lax.rem(e, 2), lax.rem(e // 2, 2), e // 4
    ex, ey, ec = e + 2 - 4 * x, e + 4 - 8 * y, e + 1 - 2 * core
    ed = ex + 4 - 8 * y
    cx, cy, cd = ex + 1 - 2 * core, ey + 1 - 2 * core, ed + 1 - 2 * core

    near, far = t + 1 - 2 * lax.rem(t, 2), 3 - t
    inner = (t == 1) | (t == 2)

    load_asked = pltpu.make_async_copy(asked_hbm, asked_ref, local.at[0])
    load_record = pltpu.make_async_copy(record_hbm, record_ref, local.at[1])
    load_record.start()
    load_asked.start()
    barrier = pltpu.get_barrier_semaphore()
    for peer in ((t, ex), (t, ey), (t, ec), (near, e), (far, e)):
        pl.semaphore_signal(barrier, inc=1, device_id=peer, device_id_type=MESH)

    row_index = lax.broadcasted_iota(jnp.int32, (HALF, HALF), 0)
    lane_index = lax.broadcasted_iota(jnp.int32, (HALF, HALF), 1)
    mirror = jnp.where(row_index + lane_index == HALF - 1, 1.0, 0.0).astype(jnp.bfloat16)

    def flip_halves(tile):
        return jnp.dot(tile, mirror, preferred_element_type=jnp.float32)

    stations = traces // comps
    load_record.wait()

    def whiten(comp, carry):
        values = record_ref[comp].astype(jnp.float32)
        values = values - jnp.mean(values, axis=-1, keepdims=True)
        power_mean = jnp.mean(values * values, axis=-1, keepdims=True)
        values = values * lax.rsqrt(power_mean + 1e-06)
        for m in range(blocks_in):
            rows = pl.ds(comp * blocks_in + m, stations, stride=comps * blocks_in)
            for h in (0, 1):
                lane = m * BLOCK + h * HALF
                rows32[h, rows, :] = values[:, lane : lane + HALF]
        return carry

    lax.fori_loop(0, comps, whiten, 0)
    for h in (0, 1):
        blks[0][e, :, :, h * HALF : (h + 1) * HALF] = (
            flip_halves(rows32[h].astype(jnp.bfloat16))
            .astype(jnp.bfloat16)
            .reshape(traces, blocks_in, HALF)
        )
    pl.semaphore_wait(barrier, 5)

    def plane_copy(k, kind, origin, target):
        blk = blks[k]
        if kind == DIAG_A:
            ref = blk.at[origin, pl.ds(0, traces // 2)]
        elif kind == DIAG_B:
            ref = blk.at[origin, pl.ds(traces // 2, traces // 2)]
        else:
            ref = blk.at[origin]
        return pltpu.make_async_remote_copy(
            src_ref=ref, dst_ref=ref,
            send_sem=send.at[k, kind], recv_sem=recv.at[k, kind],
            device_id=(t, target), device_id_type=MESH,
        )

    def z_copy(index, source, slot, target):
        return pltpu.make_async_remote_copy(
            src_ref=blks[source].at[e], dst_ref=blks[slot].at[e],
            send_sem=zsend.at[index], recv_sem=zrecv.at[slot - 1],
            device_id=(target, e), device_id_type=MESH,
        )

    own_near = z_copy(0, 0, 1, near)
    own_far = z_copy(1, 0, 2, far)
    near_to_far = z_copy(2, 1, 3, far)
    far_to_near = z_copy(3, 2, 2, near)
    rest_to_near = z_copy(4, 3, 3, near)

    def wait_window(k):
        z_copy(0, 0, k, near).wait_recv()

    def send_own(k):
        plane_copy(k, FROM_X, e, ex).start()
        plane_copy(k, FROM_Y, e, ey).start()
        plane_copy(k, CORE_OWN, e, ec).start()

    def forward_xy(k):
        plane_copy(k, FROM_X, ex, ex).wait_recv()
        plane_copy(k, DIAG_A, ex, ey).start()
        plane_copy(k, CORE_X, ex, ec).start()
        plane_copy(k, FROM_Y, ey, ey).wait_recv()
        plane_copy(k, DIAG_B, ey, ex).start()
        plane_copy(k, CORE_Y, ey, ec).start()

    def forward_diag(k):
        plane_copy(k, DIAG_A, ed, ey).wait_recv()
        plane_copy(k, DIAG_B, ed, ex).wait_recv()
        plane_copy(k, CORE_D, ed, ec).start()

    def wait_core(k):
        plane_copy(k, CORE_OWN, ec, ec).wait_recv()
        plane_copy(k, CORE_X, cx, ec).wait_recv()
        plane_copy(k, CORE_Y, cy, ec).wait_recv()
        plane_copy(k, CORE_D, cd, ec).wait_recv()

    below = lane_index <= row_index
    nothing = jnp.zeros((HALF, HALF), jnp.bfloat16)
    first_chunk = 2 * first_s

    last_chunk = 2 * last_s + 2

    def unmirror(k):
        for j in range(own_count):
            for h in (0, 1):
                lanes = slice(h * HALF, (h + 1) * HALF)
                own32[j, :, lanes] = flip_halves(blks[k][e, own_count * t + j, :, lanes])

    def build(n):
        def one(j, carry):
            index = own_count * n + j

            def eight_blocks(g, before):
                rows = own32[j, pl.ds(pl.multiple_of(8 * g, 8), 8), :]
                for b in range(8):
                    m = 8 * g + b
                    for half in (0, 1):
                        row = rows[b : b + 1, half * HALF : (half + 1) * HALF]
                        skewed = pltpu.roll(
                            jnp.broadcast_to(row, (16, HALF)), 1, 1, stride=1, stride_axis=0
                        ).astype(jnp.bfloat16)
                        now = jnp.concatenate(
                            [skewed] + [pltpu.roll(skewed, 16 * a, 1) for a in range(1, HALF // 16)],
                            axis=0,
                        )
                        lane = (2 * m + half + lag_blocks - 1 - first_chunk) * HALF
                        hankel[index, :, pl.ds(pl.multiple_of(lane, HALF), HALF)] = jnp.where(
                            below, before, now
                        )
                        before = now
                return before

            before = lax.fori_loop(0, blocks_in // 8, eight_blocks, nothing)
            lane = (2 * blocks_in + lag_blocks - 1 - first_chunk) * HALF
            hankel[index, :, lane : lane + HALF] = jnp.where(below, before, nothing)
            hankel[index, :, :HALF] = nothing
            lane = (last_chunk - first_chunk) * HALF
            hankel[index, :, lane : lane + HALF] = nothing
            return carry

        lax.fori_loop(0, own_count, one, 0)

    def pick(k):
        blk = blks[k]

        def one(slot, carry):
            d, i = slot // capacity, lax.rem(slot, capacity)
            station = asked_ref[e, i, d]
            rows = (
                blk[d, pl.ds(station * comps, comps)]
                .astype(jnp.float32)
                .reshape(comps * blocks_in, BLOCK)
            )
            start = pl.multiple_of(slot * (comps * blocks_in), comps * blocks_in)
            for h in (0, 1):
                pool32[h, pl.ds(start, comps * blocks_in), :] = rows[:, h * HALF : (h + 1) * HALF]
            return carry

        lax.fori_loop(0, owners * capacity, one, 0)

    def correlate(n):
        for m in range(blocks_in):
            for h in (0, 1):
                part = pool32[h, pl.ds(m, pool, stride=blocks_in), :].astype(jnp.bfloat16)
                pool16[m, :, h * HALF : (h + 1) * HALF] = part

        pl.when(n == 2)(functools.partial(forward_diag, 3))
        empty = jnp.zeros((pool, BLOCK), jnp.bfloat16)
        left = jnp.concatenate(
            [
                jnp.concatenate(
                    [
                        pool16[s - q] if 0 <= s - q < blocks_in else empty
                        for s in range(first_s, last_s + 1)
                    ],
                    axis=1,
                )
                for q in reversed(range(lag_blocks))
            ],
            axis=0,
        )
        right = jnp.concatenate(
            [
                jnp.concatenate(
                    [hankel[own_count * n + j, :, lane : lane + BLOCK] for j in range(own_count)], axis=1
                )
                for s in range(first_s, last_s + 1)
                for lane in ((2 * s - first_chunk) * HALF, (2 * s + 1 - first_chunk) * HALF)
            ],
            axis=0,
        )
        term = jnp.dot(left, right, preferred_element_type=jnp.float32)

        @pl.when(n == 0)
        def _():
            for j in range(own_count):
                cc_ref[j] = term[:, j * BLOCK : (j + 1) * BLOCK]

        @pl.when(n > 0)
        def _():
            for j in range(own_count):
                cc_ref[j] += term[:, j * BLOCK : (j + 1) * BLOCK]

    own_near.start()

    @pl.when(inner)
    def _():
        own_far.start()

    send_own(0)
    def before_build(n):
        if n == 1:
            wait_window(1)

            @pl.when(inner)
            def _():
                near_to_far.start()
                wait_window(2)
                far_to_near.start()

            send_own(1)
            forward_xy(0)
        if n == 2:
            forward_diag(0)

            @pl.when(jnp.logical_not(inner))
            def _():
                wait_window(2)

            @pl.when(inner)
            def _():
                wait_window(3)
                rest_to_near.start()

            send_own(2)
            forward_xy(1)
            load_asked.wait()
        if n == 3:
            forward_diag(1)

            @pl.when(jnp.logical_not(inner))
            def _():
                wait_window(3)

            send_own(3)
            forward_xy(2)
        if n == 4:
            forward_diag(2)
            forward_xy(3)
        if n < 4:
            unmirror(n)

    def before_correlate(n):
        wait_core(n)
        pick(n)

    def step(n, carry):
        for k in range(5):
            pl.when(n == k)(functools.partial(before_build, k))
        pl.when(n < 4)(functools.partial(build, n))
        for k in range(4):
            pl.when(n == k + 2)(functools.partial(before_correlate, k))
        pl.when(n >= 2)(functools.partial(correlate, n - 2))
        return carry

    lax.fori_loop(0, 6, step, 0)

    own_near.wait_send()

    @pl.when(inner)
    def _():
        own_far.wait_send()
        near_to_far.wait_send()
        far_to_near.wait_send()
        rest_to_near.wait_send()

    for k in range(4):
        plane_copy(k, FROM_X, e, ex).wait_send()
        plane_copy(k, FROM_Y, e, ey).wait_send()
        plane_copy(k, CORE_OWN, e, ec).wait_send()
        plane_copy(k, DIAG_A, ex, ey).wait_send()
        plane_copy(k, CORE_X, ex, ec).wait_send()
        plane_copy(k, DIAG_B, ey, ex).wait_send()
        plane_copy(k, CORE_Y, ey, ec).wait_send()
        plane_copy(k, CORE_D, ed, ec).wait_send()


def select_kernel(scale, own_count, comps, lag_blocks, counts_ref, partners_ref, codes_ref, cc_ref, out_ref):
    pool = cc_ref.shape[1] // lag_blocks
    slots = partners_ref.shape[2]
    pool_row = lax.broadcasted_iota(jnp.int32, (pool, slots), 0)
    slot_lane = lax.broadcasted_iota(jnp.int32, (pool, slots), 1)
    dims = (((0,), (0,)), ((), ()))

    def one(j, carry):
        trace = own_count * lax.axis_index("tm") + j
        wanted = partners_ref[trace] * comps + codes_ref[trace]
        hit = (wanted == pool_row) & (slot_lane < counts_ref[0, trace])
        chosen = jnp.where(hit, 1.0, 0.0).astype(jnp.bfloat16)
        rows = pl.ds(pl.multiple_of(j * slots, 8), slots)
        for q in range(lag_blocks):
            part = cc_ref[j, q * pool : (q + 1) * pool, :]
            high = part.astype(jnp.bfloat16)
            low = (part - high.astype(jnp.float32)).astype(jnp.bfloat16)
            total = lax.dot_general(chosen, low, dims, preferred_element_type=jnp.float32)
            total += lax.dot_general(chosen, high, dims, preferred_element_type=jnp.float32)
            lag = (lag_blocks - 1 - q) * BLOCK
            out_ref[0, rows, lag : lag + BLOCK] = total * scale
        return carry

    lax.fori_loop(0, own_count, one, 0)


def gathered_shards(record, requested, partners, codes, counts):
    stations, comps, _, window_len = record.shape
    owners, capacity = requested.shape[1:]
    traces = stations * comps
    windows = lax.axis_size("tm")
    own_count = traces // windows
    blocks_in, lag_blocks = window_len // BLOCK, LAGS // BLOCK
    pool = owners * capacity * comps
    depth = (blocks_in + lag_blocks - 3) * BLOCK
    slots = partners.shape[2]
    cc_shape = jax.ShapeDtypeStruct((own_count, lag_blocks * pool, BLOCK), jnp.float32)
    dims = (traces, blocks_in, owners, capacity, comps, own_count, lag_blocks)
    vmem = pl.BlockSpec(memory_space=pltpu.VMEM)
    smem = pl.BlockSpec(memory_space=pltpu.SMEM)
    cc = pl.pallas_call(
        functools.partial(exchange_kernel, dims),
        out_shape=cc_shape,
        in_specs=[pl.BlockSpec(memory_space=pltpu.HBM)] * 2,
        out_specs=vmem,
        scratch_shapes=[pltpu.VMEM((owners, traces, blocks_in, BLOCK), jnp.bfloat16)] * 4
        + [
            pltpu.SMEM((owners, capacity, owners), jnp.int32),
            pltpu.VMEM((comps, stations, window_len), jnp.bfloat16),
            pltpu.VMEM((2, traces * blocks_in, HALF), jnp.float32),
            pltpu.VMEM((2, pool * blocks_in, HALF), jnp.float32),
            pltpu.VMEM((own_count, blocks_in, BLOCK), jnp.float32),
            pltpu.VMEM((blocks_in, pool, BLOCK), jnp.bfloat16),
            pltpu.VMEM((4 * own_count, HALF, depth + HALF), jnp.bfloat16),
            pltpu.SemaphoreType.DMA((4, 8)),
            pltpu.SemaphoreType.DMA((4, 8)),
            pltpu.SemaphoreType.DMA((5,)),
            pltpu.SemaphoreType.DMA((3,)),
            pltpu.SemaphoreType.DMA((2,)),
        ],
        compiler_params=pltpu.CompilerParams(
            collective_id=0, has_side_effects=True, vmem_limit_bytes=60 * 1024 * 1024
        ),
    )(requested.transpose(0, 2, 1), record.transpose(2, 1, 0, 3)[0])
    return pl.pallas_call(
        functools.partial(
            select_kernel, 1.0 / math.sqrt(window_len * windows), own_count, comps, lag_blocks
        ),
        out_shape=jax.ShapeDtypeStruct((1, own_count * slots, LAGS), jnp.float32),
        in_specs=[smem, vmem, vmem, vmem],
        out_specs=vmem,
        compiler_params=pltpu.CompilerParams(vmem_limit_bytes=60 * 1024 * 1024),
    )(counts, partners.transpose(1, 0, 2), codes.transpose(1, 0, 2), cc)


def solution(mesh):
    def body(record, requested, partners, codes, counts):
        planes = lax.axis_size("tm") == 4 and lax.axis_size("pairs") == 8
        stations, comps, window_count, window_len = record.shape
        fits = (
            window_count == 1
            and stations == 4
            and window_len % (8 * BLOCK) == 0
            and LAGS == 4 * BLOCK
        )
        form = gathered_shards if planes and fits else shards
        return form(record, requested, partners, codes, counts)

    return jax.shard_map(
        body,
        mesh=mesh,
        in_specs=(
            P("pairs", None, "tm", None),
            P(),
            P("pairs", None, None),
            P("pairs", None, None),
            P("pairs", None),
        ),
        out_specs=P("pairs", "tm", None),
        check_vma=False,
    )
```

```python
import functools
import math

import jax
import jax.numpy as jnp
from jax import lax
from jax.experimental import pallas as pl
from jax.experimental.pallas import tpu as pltpu
from jax.sharding import PartitionSpec as P

LAGS = 1024


def normalize(traces):
    values = traces.astype(jnp.float32)
    values = values - jnp.mean(values, axis=-1, keepdims=True)
    power_mean = jnp.mean(values * values, axis=-1, keepdims=True)
    return (values * lax.rsqrt(power_mean + 1e-06)).astype(jnp.bfloat16)


def correlate(own_trace, partner_rows, lag_count, block_len):
    window_len = own_trace.shape[0]
    half_lag = lag_count // 2
    padded = jnp.pad(own_trace, (half_lag, half_lag + block_len))
    length = padded.shape[0]
    spread = jnp.broadcast_to(padded, (block_len, length)).reshape(-1)
    spread = jnp.pad(spread, (0, block_len))
    skewed = spread.reshape(block_len, length + 1)[:, : window_len + lag_count]
    hankel = skewed.reshape(block_len, (window_len + lag_count) // block_len, block_len)
    blocks_in = window_len // block_len
    pieces = partner_rows.reshape(partner_rows.shape[0], blocks_in, block_len)
    outputs = []
    for offset in range(lag_count // block_len):
        window_view = hankel[:, offset : offset + blocks_in, :]
        outputs.append(
            jnp.einsum("pmi,imr->pr", pieces, window_view, preferred_element_type=jnp.float32)
        )
    return jnp.concatenate(outputs, axis=1)


def shards(record, requested, partners, codes, counts):
    whitened = normalize(record)
    local_stations, comp_count, window_count, window_len = whitened.shape
    owners = lax.axis_size("pairs")
    capacity = requested.shape[2]
    per_trace = partners.shape[2]
    trace_count = local_stations * comp_count
    block_len = math.gcd(math.gcd(128, window_len), LAGS)
    own_index = lax.axis_index("pairs")
    slot_ids = partners[0]
    comp_ids = codes[0]
    everyone = lax.all_gather(whitened, "pairs", axis=0, tiled=True)
    trace_pool = everyone.reshape(owners * local_stations * comp_count, window_count, window_len)
    asked_table = lax.dynamic_index_in_dim(requested, own_index, axis=0, keepdims=False)
    station_of = (
        asked_table + jnp.arange(owners, dtype=jnp.int32)[:, None] * local_stations
    ).reshape(-1)
    matches = slot_ids[:, :, None] == jnp.arange(owners * capacity, dtype=jnp.int32)[None, None, :]
    stations = jnp.sum(jnp.where(matches, station_of[None, None, :], 0), axis=-1)
    row_ids = stations * comp_count + comp_ids
    picked = jnp.take(trace_pool, row_ids.reshape(-1), axis=0)
    live_rows = jnp.arange(per_trace, dtype=jnp.int32)[None, :] < counts[0][:, None]
    picked = jnp.where(live_rows.reshape(-1)[:, None, None], picked, jnp.zeros((), jnp.bfloat16))
    picked = picked.reshape(trace_count, per_trace, window_count, window_len)
    picked = jnp.moveaxis(picked, 2, 1).reshape(trace_count * window_count, per_trace, window_len)
    own_rows = whitened.reshape(trace_count * window_count, window_len)

    def one_trace(operands):
        own_row, partner_rows = operands
        return correlate(own_row, partner_rows, LAGS, block_len)

    lagged = lax.map(one_trace, (own_rows, picked))
    lagged = lagged.reshape(trace_count, window_count, per_trace, LAGS)
    total_windows = window_count * lax.axis_size("tm")
    window_term = jnp.sum(lagged, axis=1) * (1.0 / math.sqrt(window_len * total_windows))
    window_term = window_term.reshape(1, trace_count * per_trace, LAGS)
    return lax.psum_scatter(window_term, "tm", scatter_dimension=1, tiled=True)


MESH = pl.DeviceIdType.MESH
HALF = 128
BLOCK = 2 * HALF
X_A, X_B, Y_A, Y_B, DIAG_A, DIAG_B, CORE_OWN, CORE_X, CORE_Y, CORE_D = range(10)


def exchange_kernel(
    dims, asked_hbm, record_hbm, cc_ref, *scratch
):
    traces, blocks_in, owners, capacity, comps, own_count, lag_blocks = dims
    blks = scratch[:4]
    (asked_ref, record_ref, rows32, pool32, own32, pool16, hankel) = scratch[4:11]
    (send, recv, zsend, zrecv, local) = scratch[11:]
    pool = owners * capacity * comps
    first_s, last_s = 1, blocks_in + lag_blocks - 3
    t = lax.axis_index("tm")
    e = lax.axis_index("pairs")
    core, x, y = lax.rem(e, 2), lax.rem(e // 2, 2), e // 4
    ex, ey, ec = e + 2 - 4 * x, e + 4 - 8 * y, e + 1 - 2 * core
    ed = ex + 4 - 8 * y
    cx, cy, cd = ex + 1 - 2 * core, ey + 1 - 2 * core, ed + 1 - 2 * core

    near, far = t + 1 - 2 * lax.rem(t, 2), 3 - t
    inner = (t == 1) | (t == 2)

    load_asked = pltpu.make_async_copy(asked_hbm, asked_ref, local.at[0])
    load_record = pltpu.make_async_copy(record_hbm, record_ref, local.at[1])
    load_record.start()
    load_asked.start()
    barrier = pltpu.get_barrier_semaphore()
    for peer in ((t, ex), (t, ey), (t, ec), (near, e), (far, e)):
        pl.semaphore_signal(barrier, inc=1, device_id=peer, device_id_type=MESH)

    row_index = lax.broadcasted_iota(jnp.int32, (HALF, HALF), 0)
    lane_index = lax.broadcasted_iota(jnp.int32, (HALF, HALF), 1)
    mirror = jnp.where(row_index + lane_index == HALF - 1, 1.0, 0.0).astype(jnp.bfloat16)

    def flip_halves(tile):
        return jnp.dot(tile, mirror, preferred_element_type=jnp.float32)

    stations = traces // comps
    load_record.wait()

    def whiten(comp, carry):
        values = record_ref[comp].astype(jnp.float32)
        values = values - jnp.mean(values, axis=-1, keepdims=True)
        power_mean = jnp.mean(values * values, axis=-1, keepdims=True)
        values = values * lax.rsqrt(power_mean + 1e-06)
        for m in range(blocks_in):
            rows = pl.ds(comp * blocks_in + m, stations, stride=comps * blocks_in)
            for h in (0, 1):
                lane = m * BLOCK + h * HALF
                rows32[h, rows, :] = values[:, lane : lane + HALF]
        return carry

    lax.fori_loop(0, comps, whiten, 0)
    for h in (0, 1):
        blks[0][e, :, :, h * HALF : (h + 1) * HALF] = (
            flip_halves(rows32[h].astype(jnp.bfloat16))
            .astype(jnp.bfloat16)
            .reshape(traces, blocks_in, HALF)
        )
    pl.semaphore_wait(barrier, 5)

    def plane_copy(k, kind, origin, target):
        blk = blks[k]
        if kind in (X_A, Y_A, DIAG_A):
            ref = blk.at[origin, pl.ds(0, traces // 2)]
        elif kind in (X_B, Y_B, DIAG_B):
            ref = blk.at[origin, pl.ds(traces // 2, traces // 2)]
        else:
            ref = blk.at[origin]
        return pltpu.make_async_remote_copy(
            src_ref=ref, dst_ref=ref,
            send_sem=send.at[k, kind], recv_sem=recv.at[k, kind],
            device_id=(t, target), device_id_type=MESH,
        )

    def z_copies(index, source, slot, target):
        halves = []
        for half in (0, 1):
            part = pl.ds(half * (traces // 2), traces // 2)
            halves.append(
                pltpu.make_async_remote_copy(
                    src_ref=blks[source].at[e, part], dst_ref=blks[slot].at[e, part],
                    send_sem=zsend.at[index, half], recv_sem=zrecv.at[slot - 1, half],
                    device_id=(target, e), device_id_type=MESH,
                )
            )
        return halves

    own_near = z_copies(0, 0, 1, near)
    own_far = z_copies(1, 0, 2, far)
    near_to_far = z_copies(2, 1, 3, far)
    far_to_near = z_copies(3, 2, 2, near)
    rest_to_near = z_copies(4, 3, 3, near)

    def wait_half(k, half):
        z_copies(0, 0, k, near)[half].wait_recv()

    def send_half(k, half):
        plane_copy(k, (X_A, X_B)[half], e, ex).start()
        plane_copy(k, (Y_A, Y_B)[half], e, ey).start()

    def send_core(k):
        plane_copy(k, CORE_OWN, e, ec).start()

    def forward_xy(k):
        plane_copy(k, X_A, ex, ex).wait_recv()
        plane_copy(k, DIAG_A, ex, ey).start()
        plane_copy(k, Y_A, ey, ey).wait_recv()
        plane_copy(k, Y_B, ey, ey).wait_recv()
        plane_copy(k, DIAG_B, ey, ex).start()
        plane_copy(k, CORE_Y, ey, ec).start()
        plane_copy(k, X_B, ex, ex).wait_recv()
        plane_copy(k, CORE_X, ex, ec).start()

    def forward_diag(k):
        plane_copy(k, DIAG_A, ed, ey).wait_recv()
        plane_copy(k, DIAG_B, ed, ex).wait_recv()
        plane_copy(k, CORE_D, ed, ec).start()

    def wait_core(k):
        plane_copy(k, CORE_OWN, ec, ec).wait_recv()
        plane_copy(k, CORE_X, cx, ec).wait_recv()
        plane_copy(k, CORE_Y, cy, ec).wait_recv()
        plane_copy(k, CORE_D, cd, ec).wait_recv()

    below = lane_index <= row_index
    nothing = jnp.zeros((HALF, HALF), jnp.bfloat16)
    first_chunk = 2 * first_s

    last_chunk = 2 * last_s + 2

    def unmirror(k):
        for j in range(own_count):
            for h in (0, 1):
                lanes = slice(h * HALF, (h + 1) * HALF)
                own32[j, :, lanes] = flip_halves(blks[k][e, own_count * t + j, :, lanes])

    def build(n):
        def one(j, carry):
            index = own_count * n + j

            def eight_blocks(g, before):
                rows = own32[j, pl.ds(pl.multiple_of(8 * g, 8), 8), :]
                for b in range(8):
                    m = 8 * g + b
                    for half in (0, 1):
                        row = rows[b : b + 1, half * HALF : (half + 1) * HALF]
                        skewed = pltpu.roll(
                            jnp.broadcast_to(row, (16, HALF)), 1, 1, stride=1, stride_axis=0
                        ).astype(jnp.bfloat16)
                        now = jnp.concatenate(
                            [skewed] + [pltpu.roll(skewed, 16 * a, 1) for a in range(1, HALF // 16)],
                            axis=0,
                        )
                        lane = (2 * m + half + lag_blocks - 1 - first_chunk) * HALF
                        hankel[index, :, pl.ds(pl.multiple_of(lane, HALF), HALF)] = jnp.where(
                            below, before, now
                        )
                        before = now
                return before

            before = lax.fori_loop(0, blocks_in // 8, eight_blocks, nothing)
            lane = (2 * blocks_in + lag_blocks - 1 - first_chunk) * HALF
            hankel[index, :, lane : lane + HALF] = jnp.where(below, before, nothing)
            hankel[index, :, :HALF] = nothing
            lane = (last_chunk - first_chunk) * HALF
            hankel[index, :, lane : lane + HALF] = nothing
            return carry

        lax.fori_loop(0, own_count, one, 0)

    def pick(k):
        blk = blks[k]

        def one(slot, carry):
            d, i = slot // capacity, lax.rem(slot, capacity)
            station = asked_ref[e, i, d]
            rows = (
                blk[d, pl.ds(station * comps, comps)]
                .astype(jnp.float32)
                .reshape(comps * blocks_in, BLOCK)
            )
            start = pl.multiple_of(slot * (comps * blocks_in), comps * blocks_in)
            for h in (0, 1):
                pool32[h, pl.ds(start, comps * blocks_in), :] = rows[:, h * HALF : (h + 1) * HALF]
            return carry

        lax.fori_loop(0, owners * capacity, one, 0)

    def correlate(n):
        for m in range(blocks_in):
            for h in (0, 1):
                part = pool32[h, pl.ds(m, pool, stride=blocks_in), :].astype(jnp.bfloat16)
                pool16[m, :, h * HALF : (h + 1) * HALF] = part

        pl.when(n == 0)(functools.partial(forward_diag, 1))
        pl.when(n == 1)(functools.partial(forward_xy, 3))
        empty = jnp.zeros((pool, BLOCK), jnp.bfloat16)
        left = jnp.concatenate(
            [
                jnp.concatenate(
                    [
                        pool16[s - q] if 0 <= s - q < blocks_in else empty
                        for s in range(first_s, last_s + 1)
                    ],
                    axis=1,
                )
                for q in reversed(range(lag_blocks))
            ],
            axis=0,
        )
        right = jnp.concatenate(
            [
                jnp.concatenate(
                    [hankel[own_count * n + j, :, lane : lane + BLOCK] for j in range(own_count)], axis=1
                )
                for s in range(first_s, last_s + 1)
                for lane in ((2 * s - first_chunk) * HALF, (2 * s + 1 - first_chunk) * HALF)
            ],
            axis=0,
        )
        term = jnp.dot(left, right, preferred_element_type=jnp.float32)

        @pl.when(n == 0)
        def _():
            for j in range(own_count):
                cc_ref[j] = term[:, j * BLOCK : (j + 1) * BLOCK]

        @pl.when(n > 0)
        def _():
            for j in range(own_count):
                cc_ref[j] += term[:, j * BLOCK : (j + 1) * BLOCK]

    for half in (0, 1):
        own_near[half].start()
        send_half(0, half)

        @pl.when(inner)
        def _():
            own_far[half].start()

    send_core(0)

    def before_build(n):
        if n == 1:
            for half in (0, 1):
                wait_half(1, half)
                send_half(1, half)

                @pl.when(inner)
                def _():
                    near_to_far[half].start()
                    wait_half(2, half)
                    far_to_near[half].start()

            send_core(1)
            forward_xy(0)
        if n == 2:
            for half in (0, 1):

                @pl.when(jnp.logical_not(inner))
                def _():
                    wait_half(2, half)

                @pl.when(inner)
                def _():
                    wait_half(3, half)
                    rest_to_near[half].start()

                send_half(2, half)
            send_core(2)
            forward_diag(0)
            forward_xy(1)
        if n == 3:
            forward_xy(2)
        if n == 4:
            forward_diag(3)
        if n < 4:
            unmirror(n)

    def before_correlate(n):
        if n == 0:
            for half in (0, 1):

                @pl.when(jnp.logical_not(inner))
                def _():
                    wait_half(3, half)

                send_half(3, half)
            send_core(3)
            load_asked.wait()
        if n == 1:
            forward_diag(2)
        wait_core(n)
        pick(n)

    def step(n, carry):
        for k in range(5):
            pl.when(n == k)(functools.partial(before_build, k))
        pl.when(n < 4)(functools.partial(build, n))
        for k in range(4):
            pl.when(n == k + 2)(functools.partial(before_correlate, k))
        pl.when(n >= 2)(functools.partial(correlate, n - 2))
        return carry

    lax.fori_loop(0, 6, step, 0)

    for half in (0, 1):
        own_near[half].wait_send()

        @pl.when(inner)
        def _():
            own_far[half].wait_send()
            near_to_far[half].wait_send()
            far_to_near[half].wait_send()
            rest_to_near[half].wait_send()

    for k in range(4):
        plane_copy(k, X_A, e, ex).wait_send()
        plane_copy(k, X_B, e, ex).wait_send()
        plane_copy(k, Y_A, e, ey).wait_send()
        plane_copy(k, Y_B, e, ey).wait_send()
        plane_copy(k, CORE_OWN, e, ec).wait_send()
        plane_copy(k, DIAG_A, ex, ey).wait_send()
        plane_copy(k, CORE_X, ex, ec).wait_send()
        plane_copy(k, DIAG_B, ey, ex).wait_send()
        plane_copy(k, CORE_Y, ey, ec).wait_send()
        plane_copy(k, CORE_D, ed, ec).wait_send()


def select_kernel(scale, own_count, comps, lag_blocks, counts_ref, partners_ref, codes_ref, cc_ref, out_ref):
    pool = cc_ref.shape[1] // lag_blocks
    slots = partners_ref.shape[2]
    pool_row = lax.broadcasted_iota(jnp.int32, (pool, slots), 0)
    slot_lane = lax.broadcasted_iota(jnp.int32, (pool, slots), 1)
    dims = (((0,), (0,)), ((), ()))

    def one(j, carry):
        trace = own_count * lax.axis_index("tm") + j
        wanted = partners_ref[trace] * comps + codes_ref[trace]
        hit = (wanted == pool_row) & (slot_lane < counts_ref[0, trace])
        chosen = jnp.where(hit, 1.0, 0.0).astype(jnp.bfloat16)
        rows = pl.ds(pl.multiple_of(j * slots, 8), slots)
        for q in range(lag_blocks):
            part = cc_ref[j, q * pool : (q + 1) * pool, :]
            high = part.astype(jnp.bfloat16)
            low = (part - high.astype(jnp.float32)).astype(jnp.bfloat16)
            total = lax.dot_general(chosen, low, dims, preferred_element_type=jnp.float32)
            total += lax.dot_general(chosen, high, dims, preferred_element_type=jnp.float32)
            lag = (lag_blocks - 1 - q) * BLOCK
            out_ref[0, rows, lag : lag + BLOCK] = total * scale
        return carry

    lax.fori_loop(0, own_count, one, 0)


def gathered_shards(record, requested, partners, codes, counts):
    stations, comps, _, window_len = record.shape
    owners, capacity = requested.shape[1:]
    traces = stations * comps
    windows = lax.axis_size("tm")
    own_count = traces // windows
    blocks_in, lag_blocks = window_len // BLOCK, LAGS // BLOCK
    pool = owners * capacity * comps
    depth = (blocks_in + lag_blocks - 3) * BLOCK
    slots = partners.shape[2]
    cc_shape = jax.ShapeDtypeStruct((own_count, lag_blocks * pool, BLOCK), jnp.float32)
    dims = (traces, blocks_in, owners, capacity, comps, own_count, lag_blocks)
    vmem = pl.BlockSpec(memory_space=pltpu.VMEM)
    smem = pl.BlockSpec(memory_space=pltpu.SMEM)
    cc = pl.pallas_call(
        functools.partial(exchange_kernel, dims),
        out_shape=cc_shape,
        in_specs=[pl.BlockSpec(memory_space=pltpu.HBM)] * 2,
        out_specs=vmem,
        scratch_shapes=[pltpu.VMEM((owners, traces, blocks_in, BLOCK), jnp.bfloat16)] * 4
        + [
            pltpu.SMEM((owners, capacity, owners), jnp.int32),
            pltpu.VMEM((comps, stations, window_len), jnp.bfloat16),
            pltpu.VMEM((2, traces * blocks_in, HALF), jnp.float32),
            pltpu.VMEM((2, pool * blocks_in, HALF), jnp.float32),
            pltpu.VMEM((own_count, blocks_in, BLOCK), jnp.float32),
            pltpu.VMEM((blocks_in, pool, BLOCK), jnp.bfloat16),
            pltpu.VMEM((4 * own_count, HALF, depth + HALF), jnp.bfloat16),
            pltpu.SemaphoreType.DMA((4, 10)),
            pltpu.SemaphoreType.DMA((4, 10)),
            pltpu.SemaphoreType.DMA((5, 2)),
            pltpu.SemaphoreType.DMA((3, 2)),
            pltpu.SemaphoreType.DMA((2,)),
        ],
        compiler_params=pltpu.CompilerParams(
            collective_id=0, has_side_effects=True, vmem_limit_bytes=60 * 1024 * 1024
        ),
    )(requested.transpose(0, 2, 1), record.transpose(2, 1, 0, 3)[0])
    return pl.pallas_call(
        functools.partial(
            select_kernel, 1.0 / math.sqrt(window_len * windows), own_count, comps, lag_blocks
        ),
        out_shape=jax.ShapeDtypeStruct((1, own_count * slots, LAGS), jnp.float32),
        in_specs=[smem, vmem, vmem, vmem],
        out_specs=vmem,
        compiler_params=pltpu.CompilerParams(vmem_limit_bytes=60 * 1024 * 1024),
    )(counts, partners.transpose(1, 0, 2), codes.transpose(1, 0, 2), cc)


def solution(mesh):
    def body(record, requested, partners, codes, counts):
        planes = lax.axis_size("tm") == 4 and lax.axis_size("pairs") == 8
        stations, comps, window_count, window_len = record.shape
        fits = (
            window_count == 1
            and stations == 4
            and window_len % (8 * BLOCK) == 0
            and LAGS == 4 * BLOCK
        )
        form = gathered_shards if planes and fits else shards
        return form(record, requested, partners, codes, counts)

    return jax.shard_map(
        body,
        mesh=mesh,
        in_specs=(
            P("pairs", None, "tm", None),
            P(),
            P("pairs", None, None),
            P("pairs", None, None),
            P("pairs", None),
        ),
        out_specs=P("pairs", "tm", None),
        check_vma=False,
    )
```

```python
import functools
import math

import jax
import jax.numpy as jnp
from jax import lax
from jax.experimental import pallas as pl
from jax.experimental.pallas import tpu as pltpu
from jax.sharding import PartitionSpec as P

LAGS = 1024


def normalize(traces):
    values = traces.astype(jnp.float32)
    values = values - jnp.mean(values, axis=-1, keepdims=True)
    power_mean = jnp.mean(values * values, axis=-1, keepdims=True)
    return (values * lax.rsqrt(power_mean + 1e-06)).astype(jnp.bfloat16)


def correlate(own_trace, partner_rows, lag_count, block_len):
    window_len = own_trace.shape[0]
    half_lag = lag_count // 2
    padded = jnp.pad(own_trace, (half_lag, half_lag + block_len))
    length = padded.shape[0]
    spread = jnp.broadcast_to(padded, (block_len, length)).reshape(-1)
    spread = jnp.pad(spread, (0, block_len))
    skewed = spread.reshape(block_len, length + 1)[:, : window_len + lag_count]
    hankel = skewed.reshape(block_len, (window_len + lag_count) // block_len, block_len)
    blocks_in = window_len // block_len
    pieces = partner_rows.reshape(partner_rows.shape[0], blocks_in, block_len)
    outputs = []
    for offset in range(lag_count // block_len):
        window_view = hankel[:, offset : offset + blocks_in, :]
        outputs.append(
            jnp.einsum("pmi,imr->pr", pieces, window_view, preferred_element_type=jnp.float32)
        )
    return jnp.concatenate(outputs, axis=1)


def shards(record, requested, partners, codes, counts):
    whitened = normalize(record)
    local_stations, comp_count, window_count, window_len = whitened.shape
    owners = lax.axis_size("pairs")
    capacity = requested.shape[2]
    per_trace = partners.shape[2]
    trace_count = local_stations * comp_count
    block_len = math.gcd(math.gcd(128, window_len), LAGS)
    own_index = lax.axis_index("pairs")
    slot_ids = partners[0]
    comp_ids = codes[0]
    everyone = lax.all_gather(whitened, "pairs", axis=0, tiled=True)
    trace_pool = everyone.reshape(owners * local_stations * comp_count, window_count, window_len)
    asked_table = lax.dynamic_index_in_dim(requested, own_index, axis=0, keepdims=False)
    station_of = (
        asked_table + jnp.arange(owners, dtype=jnp.int32)[:, None] * local_stations
    ).reshape(-1)
    matches = slot_ids[:, :, None] == jnp.arange(owners * capacity, dtype=jnp.int32)[None, None, :]
    stations = jnp.sum(jnp.where(matches, station_of[None, None, :], 0), axis=-1)
    row_ids = stations * comp_count + comp_ids
    picked = jnp.take(trace_pool, row_ids.reshape(-1), axis=0)
    live_rows = jnp.arange(per_trace, dtype=jnp.int32)[None, :] < counts[0][:, None]
    picked = jnp.where(live_rows.reshape(-1)[:, None, None], picked, jnp.zeros((), jnp.bfloat16))
    picked = picked.reshape(trace_count, per_trace, window_count, window_len)
    picked = jnp.moveaxis(picked, 2, 1).reshape(trace_count * window_count, per_trace, window_len)
    own_rows = whitened.reshape(trace_count * window_count, window_len)

    def one_trace(operands):
        own_row, partner_rows = operands
        return correlate(own_row, partner_rows, LAGS, block_len)

    lagged = lax.map(one_trace, (own_rows, picked))
    lagged = lagged.reshape(trace_count, window_count, per_trace, LAGS)
    total_windows = window_count * lax.axis_size("tm")
    window_term = jnp.sum(lagged, axis=1) * (1.0 / math.sqrt(window_len * total_windows))
    window_term = window_term.reshape(1, trace_count * per_trace, LAGS)
    return lax.psum_scatter(window_term, "tm", scatter_dimension=1, tiled=True)


MESH = pl.DeviceIdType.MESH
HALF = 128
BLOCK = 2 * HALF
FROM_X, FROM_Y, DIAG_A, DIAG_B, CORE_OWN, CORE_X, CORE_Y, CORE_D = range(8)


def exchange_kernel(
    dims, asked_hbm, record_hbm, cc_ref, *scratch
):
    traces, blocks_in, owners, capacity, comps, own_count, lag_blocks = dims
    blks = scratch[:4]
    (asked_ref, record_ref, rows32, pool32, own32, pool16, hankel) = scratch[4:11]
    (send, recv, zsend, zrecv, local) = scratch[11:]
    pool = owners * capacity * comps
    first_s, last_s = 1, blocks_in + lag_blocks - 3
    t = lax.axis_index("tm")
    e = lax.axis_index("pairs")
    core, x, y = lax.rem(e, 2), lax.rem(e // 2, 2), e // 4
    ex, ey, ec = e + 2 - 4 * x, e + 4 - 8 * y, e + 1 - 2 * core
    ed = ex + 4 - 8 * y
    cx, cy, cd = ex + 1 - 2 * core, ey + 1 - 2 * core, ed + 1 - 2 * core

    near, far = t + 1 - 2 * lax.rem(t, 2), 3 - t
    inner = (t == 1) | (t == 2)

    load_asked = pltpu.make_async_copy(asked_hbm, asked_ref, local.at[0])
    load_record = pltpu.make_async_copy(record_hbm, record_ref, local.at[1])
    load_record.start()
    load_asked.start()
    barrier = pltpu.get_barrier_semaphore()
    for peer in ((t, ex), (t, ey), (t, ec), (near, e), (far, e)):
        pl.semaphore_signal(barrier, inc=1, device_id=peer, device_id_type=MESH)

    row_index = lax.broadcasted_iota(jnp.int32, (HALF, HALF), 0)
    lane_index = lax.broadcasted_iota(jnp.int32, (HALF, HALF), 1)
    mirror = jnp.where(row_index + lane_index == HALF - 1, 1.0, 0.0).astype(jnp.bfloat16)

    def flip_halves(tile):
        return jnp.dot(tile, mirror, preferred_element_type=jnp.float32)

    stations = traces // comps
    load_record.wait()

    def whiten(comp, carry):
        values = record_ref[comp].astype(jnp.float32)
        values = values - jnp.mean(values, axis=-1, keepdims=True)
        power_mean = jnp.mean(values * values, axis=-1, keepdims=True)
        values = values * lax.rsqrt(power_mean + 1e-06)
        for m in range(blocks_in):
            rows = pl.ds(comp * blocks_in + m, stations, stride=comps * blocks_in)
            for h in (0, 1):
                lane = m * BLOCK + h * HALF
                rows32[h, rows, :] = values[:, lane : lane + HALF]
        return carry

    lax.fori_loop(0, comps, whiten, 0)
    for h in (0, 1):
        blks[0][e, :, :, h * HALF : (h + 1) * HALF] = (
            flip_halves(rows32[h].astype(jnp.bfloat16))
            .astype(jnp.bfloat16)
            .reshape(traces, blocks_in, HALF)
        )
    pl.semaphore_wait(barrier, 5)

    def plane_copy(k, kind, origin, target):
        blk = blks[k]
        if kind == DIAG_A:
            ref = blk.at[origin, pl.ds(0, traces // 2)]
        elif kind == DIAG_B:
            ref = blk.at[origin, pl.ds(traces // 2, traces // 2)]
        else:
            ref = blk.at[origin]
        return pltpu.make_async_remote_copy(
            src_ref=ref, dst_ref=ref,
            send_sem=send.at[k, kind], recv_sem=recv.at[k, kind],
            device_id=(t, target), device_id_type=MESH,
        )

    def z_copy(index, source, slot, target):
        return pltpu.make_async_remote_copy(
            src_ref=blks[source].at[e], dst_ref=blks[slot].at[e],
            send_sem=zsend.at[index], recv_sem=zrecv.at[slot - 1],
            device_id=(target, e), device_id_type=MESH,
        )

    own_near = z_copy(0, 0, 1, near)
    own_far = z_copy(1, 0, 2, far)
    near_to_far = z_copy(2, 1, 3, far)
    far_to_near = z_copy(3, 2, 2, near)
    rest_to_near = z_copy(4, 3, 3, near)

    def wait_window(k):
        z_copy(0, 0, k, near).wait_recv()

    def send_own(k):
        plane_copy(k, FROM_X, e, ex).start()
        plane_copy(k, FROM_Y, e, ey).start()
        plane_copy(k, CORE_OWN, e, ec).start()

    def forward_xy(k):
        plane_copy(k, FROM_X, ex, ex).wait_recv()
        plane_copy(k, DIAG_A, ex, ey).start()
        plane_copy(k, CORE_X, ex, ec).start()
        plane_copy(k, FROM_Y, ey, ey).wait_recv()
        plane_copy(k, DIAG_B, ey, ex).start()
        plane_copy(k, CORE_Y, ey, ec).start()

    def forward_diag(k):
        plane_copy(k, DIAG_A, ed, ey).wait_recv()
        plane_copy(k, DIAG_B, ed, ex).wait_recv()
        plane_copy(k, CORE_D, ed, ec).start()

    def wait_core(k):
        plane_copy(k, CORE_OWN, ec, ec).wait_recv()
        plane_copy(k, CORE_X, cx, ec).wait_recv()
        plane_copy(k, CORE_Y, cy, ec).wait_recv()
        plane_copy(k, CORE_D, cd, ec).wait_recv()

    below = lane_index <= row_index
    nothing = jnp.zeros((HALF, HALF), jnp.bfloat16)
    first_chunk = 2 * first_s

    last_chunk = 2 * last_s + 2

    def unmirror(k):
        for h in (0, 1):
            lanes = slice(h * HALF, (h + 1) * HALF)
            own = blks[k][e, pl.ds(own_count * t, own_count), :, lanes]
            flipped = flip_halves(own.reshape(own_count * blocks_in, HALF))
            own32[:, :, lanes] = flipped.reshape(own_count, blocks_in, HALF)

    def build(n):
        def one(j, carry):
            index = own_count * n + j

            def eight_blocks(g, before):
                rows = own32[j, pl.ds(pl.multiple_of(8 * g, 8), 8), :]
                for b in range(8):
                    m = 8 * g + b
                    for half in (0, 1):
                        row = rows[b : b + 1, half * HALF : (half + 1) * HALF]
                        skewed = pltpu.roll(
                            jnp.broadcast_to(row, (16, HALF)), 1, 1, stride=1, stride_axis=0
                        ).astype(jnp.bfloat16)
                        now = jnp.concatenate(
                            [skewed] + [pltpu.roll(skewed, 16 * a, 1) for a in range(1, HALF // 16)],
                            axis=0,
                        )
                        lane = (2 * m + half + lag_blocks - 1 - first_chunk) * HALF
                        hankel[index, :, pl.ds(pl.multiple_of(lane, HALF), HALF)] = jnp.where(
                            below, before, now
                        )
                        before = now
                return before

            before = lax.fori_loop(0, blocks_in // 8, eight_blocks, nothing)
            lane = (2 * blocks_in + lag_blocks - 1 - first_chunk) * HALF
            hankel[index, :, lane : lane + HALF] = jnp.where(below, before, nothing)
            hankel[index, :, :HALF] = nothing
            lane = (last_chunk - first_chunk) * HALF
            hankel[index, :, lane : lane + HALF] = nothing
            return carry

        lax.fori_loop(0, own_count, one, 0)

    def pick(k):
        blk = blks[k]

        def one(slot, carry):
            d, i = slot // capacity, lax.rem(slot, capacity)
            station = asked_ref[e, i, d]
            rows = (
                blk[d, pl.ds(station * comps, comps)]
                .astype(jnp.float32)
                .reshape(comps * blocks_in, BLOCK)
            )
            start = pl.multiple_of(slot * (comps * blocks_in), comps * blocks_in)
            for h in (0, 1):
                pool32[h, pl.ds(start, comps * blocks_in), :] = rows[:, h * HALF : (h + 1) * HALF]
            return carry

        lax.fori_loop(0, owners * capacity, one, 0, unroll=4)

    def correlate(n):
        for m in range(blocks_in):
            for h in (0, 1):
                part = pool32[h, pl.ds(m, pool, stride=blocks_in), :].astype(jnp.bfloat16)
                pool16[m, :, h * HALF : (h + 1) * HALF] = part

        pl.when(n == 2)(functools.partial(forward_diag, 3))
        empty = jnp.zeros((pool, BLOCK), jnp.bfloat16)
        left = jnp.concatenate(
            [
                jnp.concatenate(
                    [
                        pool16[s - q] if 0 <= s - q < blocks_in else empty
                        for s in range(first_s, last_s + 1)
                    ],
                    axis=1,
                )
                for q in reversed(range(lag_blocks))
            ],
            axis=0,
        )
        right = jnp.concatenate(
            [
                jnp.concatenate(
                    [hankel[own_count * n + j, :, lane : lane + BLOCK] for j in range(own_count)], axis=1
                )
                for s in range(first_s, last_s + 1)
                for lane in ((2 * s - first_chunk) * HALF, (2 * s + 1 - first_chunk) * HALF)
            ],
            axis=0,
        )
        term = jnp.dot(left, right, preferred_element_type=jnp.float32)

        @pl.when(n == 0)
        def _():
            for j in range(own_count):
                cc_ref[j] = term[:, j * BLOCK : (j + 1) * BLOCK]

        @pl.when(n > 0)
        def _():
            for j in range(own_count):
                cc_ref[j] += term[:, j * BLOCK : (j + 1) * BLOCK]

    own_near.start()

    @pl.when(inner)
    def _():
        own_far.start()

    send_own(0)
    def before_build(n):
        if n == 1:
            wait_window(1)

            @pl.when(inner)
            def _():
                near_to_far.start()
                wait_window(2)
                far_to_near.start()

            send_own(1)
            forward_xy(0)
        if n == 2:
            forward_diag(0)

            @pl.when(jnp.logical_not(inner))
            def _():
                wait_window(2)

            @pl.when(inner)
            def _():
                wait_window(3)
                rest_to_near.start()

            send_own(2)
            forward_xy(1)
            load_asked.wait()
        if n == 3:
            forward_diag(1)

            @pl.when(jnp.logical_not(inner))
            def _():
                wait_window(3)

            send_own(3)
            forward_xy(2)
        if n == 4:
            forward_diag(2)
            forward_xy(3)
        if n < 4:
            unmirror(n)

    def before_correlate(n):
        wait_core(n)
        pick(n)

    def step(n, carry):
        for k in range(5):
            pl.when(n == k)(functools.partial(before_build, k))
        pl.when(n < 4)(functools.partial(build, n))
        for k in range(4):
            pl.when(n == k + 2)(functools.partial(before_correlate, k))
        pl.when(n >= 2)(functools.partial(correlate, n - 2))
        return carry

    lax.fori_loop(0, 6, step, 0)

    own_near.wait_send()

    @pl.when(inner)
    def _():
        own_far.wait_send()
        near_to_far.wait_send()
        far_to_near.wait_send()
        rest_to_near.wait_send()

    for k in range(4):
        plane_copy(k, FROM_X, e, ex).wait_send()
        plane_copy(k, FROM_Y, e, ey).wait_send()
        plane_copy(k, CORE_OWN, e, ec).wait_send()
        plane_copy(k, DIAG_A, ex, ey).wait_send()
        plane_copy(k, CORE_X, ex, ec).wait_send()
        plane_copy(k, DIAG_B, ey, ex).wait_send()
        plane_copy(k, CORE_Y, ey, ec).wait_send()
        plane_copy(k, CORE_D, ed, ec).wait_send()


def select_kernel(scale, own_count, comps, lag_blocks, counts_ref, partners_ref, codes_ref, cc_hbm, out_hbm, cc_ref, out_ref, fetched, written):
    fetches = [
        pltpu.make_async_copy(cc_hbm.at[j], cc_ref.at[j], fetched.at[j]) for j in range(own_count)
    ]
    for fetch in fetches:
        fetch.start()
    writes = []
    pool = cc_ref.shape[1] // lag_blocks
    slots = partners_ref.shape[2]
    pool_row = lax.broadcasted_iota(jnp.int32, (pool, slots), 0)
    slot_lane = lax.broadcasted_iota(jnp.int32, (pool, slots), 1)
    dims = (((0,), (0,)), ((), ()))

    for j in range(own_count):
        trace = own_count * lax.axis_index("tm") + j
        wanted = partners_ref[trace] * comps + codes_ref[trace]
        hit = (wanted == pool_row) & (slot_lane < counts_ref[0, trace])
        chosen = jnp.where(hit, 1.0, 0.0).astype(jnp.bfloat16)
        fetches[j].wait()
        for q in range(lag_blocks):
            part = cc_ref[j, q * pool : (q + 1) * pool, :]
            high = part.astype(jnp.bfloat16)
            low = (part - high.astype(jnp.float32)).astype(jnp.bfloat16)
            total = lax.dot_general(chosen, low, dims, preferred_element_type=jnp.float32)
            total += lax.dot_general(chosen, high, dims, preferred_element_type=jnp.float32)
            lag = (lag_blocks - 1 - q) * BLOCK
            out_ref[j, :, lag : lag + BLOCK] = total * scale
        writes.append(
            pltpu.make_async_copy(
                out_ref.at[j], out_hbm.at[0, pl.ds(j * slots, slots)], written.at[j]
            )
        )
        writes[j].start()
    for write in writes:
        write.wait()


def gathered_shards(record, requested, partners, codes, counts):
    stations, comps, _, window_len = record.shape
    owners, capacity = requested.shape[1:]
    traces = stations * comps
    windows = lax.axis_size("tm")
    own_count = traces // windows
    blocks_in, lag_blocks = window_len // BLOCK, LAGS // BLOCK
    pool = owners * capacity * comps
    depth = (blocks_in + lag_blocks - 3) * BLOCK
    slots = partners.shape[2]
    cc_shape = jax.ShapeDtypeStruct((own_count, lag_blocks * pool, BLOCK), jnp.float32)
    dims = (traces, blocks_in, owners, capacity, comps, own_count, lag_blocks)
    vmem = pl.BlockSpec(memory_space=pltpu.VMEM)
    smem = pl.BlockSpec(memory_space=pltpu.SMEM)
    cc = pl.pallas_call(
        functools.partial(exchange_kernel, dims),
        out_shape=cc_shape,
        in_specs=[pl.BlockSpec(memory_space=pltpu.HBM)] * 2,
        out_specs=vmem,
        scratch_shapes=[pltpu.VMEM((owners, traces, blocks_in, BLOCK), jnp.bfloat16)] * 4
        + [
            pltpu.SMEM((owners, capacity, owners), jnp.int32),
            pltpu.VMEM((comps, stations, window_len), jnp.bfloat16),
            pltpu.VMEM((2, traces * blocks_in, HALF), jnp.float32),
            pltpu.VMEM((2, pool * blocks_in, HALF), jnp.float32),
            pltpu.VMEM((own_count, blocks_in, BLOCK), jnp.float32),
            pltpu.VMEM((blocks_in, pool, BLOCK), jnp.bfloat16),
            pltpu.VMEM((4 * own_count, HALF, depth + HALF), jnp.bfloat16),
            pltpu.SemaphoreType.DMA((4, 8)),
            pltpu.SemaphoreType.DMA((4, 8)),
            pltpu.SemaphoreType.DMA((5,)),
            pltpu.SemaphoreType.DMA((3,)),
            pltpu.SemaphoreType.DMA((2,)),
        ],
        compiler_params=pltpu.CompilerParams(
            collective_id=0, has_side_effects=True, vmem_limit_bytes=60 * 1024 * 1024
        ),
    )(requested.transpose(0, 2, 1), record.transpose(2, 1, 0, 3)[0])
    return pl.pallas_call(
        functools.partial(
            select_kernel, 1.0 / math.sqrt(window_len * windows), own_count, comps, lag_blocks
        ),
        out_shape=jax.ShapeDtypeStruct((1, own_count * slots, LAGS), jnp.float32),
        in_specs=[smem, vmem, vmem, pl.BlockSpec(memory_space=pltpu.HBM)],
        out_specs=pl.BlockSpec(memory_space=pltpu.HBM),
        scratch_shapes=[
            pltpu.VMEM(cc_shape.shape, jnp.float32),
            pltpu.VMEM((own_count, slots, LAGS), jnp.float32),
            pltpu.SemaphoreType.DMA((own_count,)),
            pltpu.SemaphoreType.DMA((own_count,)),
        ],
        compiler_params=pltpu.CompilerParams(vmem_limit_bytes=60 * 1024 * 1024),
    )(counts, partners.transpose(1, 0, 2), codes.transpose(1, 0, 2), cc)


def solution(mesh):
    def body(record, requested, partners, codes, counts):
        planes = lax.axis_size("tm") == 4 and lax.axis_size("pairs") == 8
        stations, comps, window_count, window_len = record.shape
        fits = (
            window_count == 1
            and stations == 4
            and window_len % (8 * BLOCK) == 0
            and LAGS == 4 * BLOCK
        )
        form = gathered_shards if planes and fits else shards
        return form(record, requested, partners, codes, counts)

    return jax.shard_map(
        body,
        mesh=mesh,
        in_specs=(
            P("pairs", None, "tm", None),
            P(),
            P("pairs", None, None),
            P("pairs", None, None),
            P("pairs", None),
        ),
        out_specs=P("pairs", "tm", None),
        check_vma=False,
    )
```

```python
import functools
import math

import jax
import jax.numpy as jnp
from jax import lax
from jax.experimental import pallas as pl
from jax.experimental.pallas import tpu as pltpu
from jax.sharding import PartitionSpec as P

LAGS = 1024


def normalize(traces):
    values = traces.astype(jnp.float32)
    values = values - jnp.mean(values, axis=-1, keepdims=True)
    power_mean = jnp.mean(values * values, axis=-1, keepdims=True)
    return (values * lax.rsqrt(power_mean + 1e-06)).astype(jnp.bfloat16)


def correlate(own_trace, partner_rows, lag_count, block_len):
    window_len = own_trace.shape[0]
    half_lag = lag_count // 2
    padded = jnp.pad(own_trace, (half_lag, half_lag + block_len))
    length = padded.shape[0]
    spread = jnp.broadcast_to(padded, (block_len, length)).reshape(-1)
    spread = jnp.pad(spread, (0, block_len))
    skewed = spread.reshape(block_len, length + 1)[:, : window_len + lag_count]
    hankel = skewed.reshape(block_len, (window_len + lag_count) // block_len, block_len)
    blocks_in = window_len // block_len
    pieces = partner_rows.reshape(partner_rows.shape[0], blocks_in, block_len)
    outputs = []
    for offset in range(lag_count // block_len):
        window_view = hankel[:, offset : offset + blocks_in, :]
        outputs.append(
            jnp.einsum("pmi,imr->pr", pieces, window_view, preferred_element_type=jnp.float32)
        )
    return jnp.concatenate(outputs, axis=1)


def shards(record, requested, partners, codes, counts):
    whitened = normalize(record)
    local_stations, comp_count, window_count, window_len = whitened.shape
    owners = lax.axis_size("pairs")
    capacity = requested.shape[2]
    per_trace = partners.shape[2]
    trace_count = local_stations * comp_count
    block_len = math.gcd(math.gcd(128, window_len), LAGS)
    own_index = lax.axis_index("pairs")
    slot_ids = partners[0]
    comp_ids = codes[0]
    everyone = lax.all_gather(whitened, "pairs", axis=0, tiled=True)
    trace_pool = everyone.reshape(owners * local_stations * comp_count, window_count, window_len)
    asked_table = lax.dynamic_index_in_dim(requested, own_index, axis=0, keepdims=False)
    station_of = (
        asked_table + jnp.arange(owners, dtype=jnp.int32)[:, None] * local_stations
    ).reshape(-1)
    matches = slot_ids[:, :, None] == jnp.arange(owners * capacity, dtype=jnp.int32)[None, None, :]
    stations = jnp.sum(jnp.where(matches, station_of[None, None, :], 0), axis=-1)
    row_ids = stations * comp_count + comp_ids
    picked = jnp.take(trace_pool, row_ids.reshape(-1), axis=0)
    live_rows = jnp.arange(per_trace, dtype=jnp.int32)[None, :] < counts[0][:, None]
    picked = jnp.where(live_rows.reshape(-1)[:, None, None], picked, jnp.zeros((), jnp.bfloat16))
    picked = picked.reshape(trace_count, per_trace, window_count, window_len)
    picked = jnp.moveaxis(picked, 2, 1).reshape(trace_count * window_count, per_trace, window_len)
    own_rows = whitened.reshape(trace_count * window_count, window_len)

    def one_trace(operands):
        own_row, partner_rows = operands
        return correlate(own_row, partner_rows, LAGS, block_len)

    lagged = lax.map(one_trace, (own_rows, picked))
    lagged = lagged.reshape(trace_count, window_count, per_trace, LAGS)
    total_windows = window_count * lax.axis_size("tm")
    window_term = jnp.sum(lagged, axis=1) * (1.0 / math.sqrt(window_len * total_windows))
    window_term = window_term.reshape(1, trace_count * per_trace, LAGS)
    return lax.psum_scatter(window_term, "tm", scatter_dimension=1, tiled=True)


MESH = pl.DeviceIdType.MESH
HALF = 128
BLOCK = 2 * HALF
FROM_X, FROM_Y, DIAG_A, DIAG_B, CORE_OWN, CORE_X, CORE_Y, CORE_D = range(8)


def exchange_kernel(
    dims, scale, asked_hbm, record_hbm, counts_hbm, partners_hbm, codes_hbm, out_ref, *scratch
):
    traces, blocks_in, owners, capacity, comps, own_count, lag_blocks = dims
    blks = scratch[:4]
    (asked_ref, record_ref, rows32, pool32, own32, pool16, hankel) = scratch[4:11]
    (send, recv, zsend, zrecv, local) = scratch[11:16]
    (cc_ref, counts_ref, partners_ref, codes_ref) = scratch[16:]
    pool = owners * capacity * comps
    first_s, last_s = 1, blocks_in + lag_blocks - 3
    t = lax.axis_index("tm")
    e = lax.axis_index("pairs")
    core, x, y = lax.rem(e, 2), lax.rem(e // 2, 2), e // 4
    ex, ey, ec = e + 2 - 4 * x, e + 4 - 8 * y, e + 1 - 2 * core
    ed = ex + 4 - 8 * y
    cx, cy, cd = ex + 1 - 2 * core, ey + 1 - 2 * core, ed + 1 - 2 * core

    near, far = t + 1 - 2 * lax.rem(t, 2), 3 - t
    inner = (t == 1) | (t == 2)

    load_asked = pltpu.make_async_copy(asked_hbm, asked_ref, local.at[0])
    load_record = pltpu.make_async_copy(record_hbm, record_ref, local.at[1])
    tables = [
        pltpu.make_async_copy(counts_hbm, counts_ref, local.at[2]),
        pltpu.make_async_copy(partners_hbm, partners_ref, local.at[3]),
        pltpu.make_async_copy(codes_hbm, codes_ref, local.at[4]),
    ]
    load_record.start()
    load_asked.start()
    for table in tables:
        table.start()
    barrier = pltpu.get_barrier_semaphore()
    for peer in ((t, ex), (t, ey), (t, ec), (near, e), (far, e)):
        pl.semaphore_signal(barrier, inc=1, device_id=peer, device_id_type=MESH)

    row_index = lax.broadcasted_iota(jnp.int32, (HALF, HALF), 0)
    lane_index = lax.broadcasted_iota(jnp.int32, (HALF, HALF), 1)
    mirror = jnp.where(row_index + lane_index == HALF - 1, 1.0, 0.0).astype(jnp.bfloat16)

    def flip_halves(tile):
        return jnp.dot(tile, mirror, preferred_element_type=jnp.float32)

    stations = traces // comps
    load_record.wait()

    def whiten(comp, carry):
        values = record_ref[comp].astype(jnp.float32)
        values = values - jnp.mean(values, axis=-1, keepdims=True)
        power_mean = jnp.mean(values * values, axis=-1, keepdims=True)
        values = values * lax.rsqrt(power_mean + 1e-06)
        for m in range(blocks_in):
            rows = pl.ds(comp * blocks_in + m, stations, stride=comps * blocks_in)
            for h in (0, 1):
                lane = m * BLOCK + h * HALF
                rows32[h, rows, :] = values[:, lane : lane + HALF]
        return carry

    lax.fori_loop(0, comps, whiten, 0)
    for h in (0, 1):
        blks[0][e, :, :, h * HALF : (h + 1) * HALF] = (
            flip_halves(rows32[h].astype(jnp.bfloat16))
            .astype(jnp.bfloat16)
            .reshape(traces, blocks_in, HALF)
        )
    pl.semaphore_wait(barrier, 5)

    def plane_copy(k, kind, origin, target):
        blk = blks[k]
        if kind == DIAG_A:
            ref = blk.at[origin, pl.ds(0, traces // 2)]
        elif kind == DIAG_B:
            ref = blk.at[origin, pl.ds(traces // 2, traces // 2)]
        else:
            ref = blk.at[origin]
        return pltpu.make_async_remote_copy(
            src_ref=ref, dst_ref=ref,
            send_sem=send.at[k, kind], recv_sem=recv.at[k, kind],
            device_id=(t, target), device_id_type=MESH,
        )

    def z_copy(index, source, slot, target):
        return pltpu.make_async_remote_copy(
            src_ref=blks[source].at[e], dst_ref=blks[slot].at[e],
            send_sem=zsend.at[index], recv_sem=zrecv.at[slot - 1],
            device_id=(target, e), device_id_type=MESH,
        )

    own_near = z_copy(0, 0, 1, near)
    own_far = z_copy(1, 0, 2, far)
    near_to_far = z_copy(2, 1, 3, far)
    far_to_near = z_copy(3, 2, 2, near)
    rest_to_near = z_copy(4, 3, 3, near)

    def wait_window(k):
        z_copy(0, 0, k, near).wait_recv()

    def send_own(k):
        plane_copy(k, FROM_X, e, ex).start()
        plane_copy(k, FROM_Y, e, ey).start()
        plane_copy(k, CORE_OWN, e, ec).start()

    def forward_xy(k):
        plane_copy(k, FROM_X, ex, ex).wait_recv()
        plane_copy(k, DIAG_A, ex, ey).start()
        plane_copy(k, CORE_X, ex, ec).start()
        plane_copy(k, FROM_Y, ey, ey).wait_recv()
        plane_copy(k, DIAG_B, ey, ex).start()
        plane_copy(k, CORE_Y, ey, ec).start()

    def forward_diag(k):
        plane_copy(k, DIAG_A, ed, ey).wait_recv()
        plane_copy(k, DIAG_B, ed, ex).wait_recv()
        plane_copy(k, CORE_D, ed, ec).start()

    def wait_core(k):
        plane_copy(k, CORE_OWN, ec, ec).wait_recv()
        plane_copy(k, CORE_X, cx, ec).wait_recv()
        plane_copy(k, CORE_Y, cy, ec).wait_recv()
        plane_copy(k, CORE_D, cd, ec).wait_recv()

    below = lane_index <= row_index
    nothing = jnp.zeros((HALF, HALF), jnp.bfloat16)
    first_chunk = 2 * first_s

    last_chunk = 2 * last_s + 2

    def unmirror(k):
        for j in range(own_count):
            for h in (0, 1):
                lanes = slice(h * HALF, (h + 1) * HALF)
                own32[j, :, lanes] = flip_halves(blks[k][e, own_count * t + j, :, lanes])

    def build(n):
        def one(j, carry):
            index = own_count * n + j

            def eight_blocks(g, before):
                rows = own32[j, pl.ds(pl.multiple_of(8 * g, 8), 8), :]
                for b in range(8):
                    m = 8 * g + b
                    for half in (0, 1):
                        row = rows[b : b + 1, half * HALF : (half + 1) * HALF]
                        skewed = pltpu.roll(
                            jnp.broadcast_to(row, (16, HALF)), 1, 1, stride=1, stride_axis=0
                        ).astype(jnp.bfloat16)
                        now = jnp.concatenate(
                            [skewed] + [pltpu.roll(skewed, 16 * a, 1) for a in range(1, HALF // 16)],
                            axis=0,
                        )
                        lane = (2 * m + half + lag_blocks - 1 - first_chunk) * HALF
                        hankel[index, :, pl.ds(pl.multiple_of(lane, HALF), HALF)] = jnp.where(
                            below, before, now
                        )
                        before = now
                return before

            before = lax.fori_loop(0, blocks_in // 8, eight_blocks, nothing)
            lane = (2 * blocks_in + lag_blocks - 1 - first_chunk) * HALF
            hankel[index, :, lane : lane + HALF] = jnp.where(below, before, nothing)
            hankel[index, :, :HALF] = nothing
            lane = (last_chunk - first_chunk) * HALF
            hankel[index, :, lane : lane + HALF] = nothing
            return carry

        lax.fori_loop(0, own_count, one, 0)

    def pick(k):
        blk = blks[k]

        def one(slot, carry):
            d, i = slot // capacity, lax.rem(slot, capacity)
            station = asked_ref[e, i, d]
            rows = (
                blk[d, pl.ds(station * comps, comps)]
                .astype(jnp.float32)
                .reshape(comps * blocks_in, BLOCK)
            )
            start = pl.multiple_of(slot * (comps * blocks_in), comps * blocks_in)
            for h in (0, 1):
                pool32[h, pl.ds(start, comps * blocks_in), :] = rows[:, h * HALF : (h + 1) * HALF]
            return carry

        lax.fori_loop(0, owners * capacity, one, 0)

    def correlate(n):
        for m in range(blocks_in):
            for h in (0, 1):
                part = pool32[h, pl.ds(m, pool, stride=blocks_in), :].astype(jnp.bfloat16)
                pool16[m, :, h * HALF : (h + 1) * HALF] = part

        pl.when(n == 2)(functools.partial(forward_diag, 3))
        empty = jnp.zeros((pool, BLOCK), jnp.bfloat16)
        left = jnp.concatenate(
            [
                jnp.concatenate(
                    [
                        pool16[s - q] if 0 <= s - q < blocks_in else empty
                        for s in range(first_s, last_s + 1)
                    ],
                    axis=1,
                )
                for q in reversed(range(lag_blocks))
            ],
            axis=0,
        )
        right = jnp.concatenate(
            [
                jnp.concatenate(
                    [hankel[own_count * n + j, :, lane : lane + BLOCK] for j in range(own_count)], axis=1
                )
                for s in range(first_s, last_s + 1)
                for lane in ((2 * s - first_chunk) * HALF, (2 * s + 1 - first_chunk) * HALF)
            ],
            axis=0,
        )
        term = jnp.dot(left, right, preferred_element_type=jnp.float32)

        @pl.when(n == 0)
        def _():
            for j in range(own_count):
                cc_ref[j] = term[:, j * BLOCK : (j + 1) * BLOCK]

        @pl.when(n > 0)
        def _():
            for j in range(own_count):
                cc_ref[j] += term[:, j * BLOCK : (j + 1) * BLOCK]

    own_near.start()

    @pl.when(inner)
    def _():
        own_far.start()

    send_own(0)
    def before_build(n):
        if n == 1:
            wait_window(1)

            @pl.when(inner)
            def _():
                near_to_far.start()
                wait_window(2)
                far_to_near.start()

            send_own(1)
            forward_xy(0)
        if n == 2:
            forward_diag(0)

            @pl.when(jnp.logical_not(inner))
            def _():
                wait_window(2)

            @pl.when(inner)
            def _():
                wait_window(3)
                rest_to_near.start()

            send_own(2)
            forward_xy(1)
            load_asked.wait()
        if n == 3:
            forward_diag(1)

            @pl.when(jnp.logical_not(inner))
            def _():
                wait_window(3)

            send_own(3)
            forward_xy(2)
        if n == 4:
            forward_diag(2)
            forward_xy(3)
        if n < 4:
            unmirror(n)

    def before_correlate(n):
        wait_core(n)
        pick(n)

    def step(n, carry):
        for k in range(5):
            pl.when(n == k)(functools.partial(before_build, k))
        pl.when(n < 4)(functools.partial(build, n))
        for k in range(4):
            pl.when(n == k + 2)(functools.partial(before_correlate, k))
        pl.when(n >= 2)(functools.partial(correlate, n - 2))
        return carry

    lax.fori_loop(0, 6, step, 0)

    for table in tables:
        table.wait()
    slots = partners_ref.shape[2]
    pool_row = lax.broadcasted_iota(jnp.int32, (pool, slots), 0)
    slot_lane = lax.broadcasted_iota(jnp.int32, (pool, slots), 1)
    dims = (((0,), (0,)), ((), ()))

    def select(j, carry):
        trace = own_count * t + j
        wanted = partners_ref[trace] * comps + codes_ref[trace]
        hit = (wanted == pool_row) & (slot_lane < counts_ref[0, trace])
        chosen = jnp.where(hit, 1.0, 0.0).astype(jnp.bfloat16)
        rows = pl.ds(pl.multiple_of(j * slots, 8), slots)
        for q in range(lag_blocks):
            part = cc_ref[j, q * pool : (q + 1) * pool, :]
            high = part.astype(jnp.bfloat16)
            low = (part - high.astype(jnp.float32)).astype(jnp.bfloat16)
            total = lax.dot_general(chosen, low, dims, preferred_element_type=jnp.float32)
            total += lax.dot_general(chosen, high, dims, preferred_element_type=jnp.float32)
            lag = (lag_blocks - 1 - q) * BLOCK
            out_ref[0, rows, lag : lag + BLOCK] = total * scale
        return carry

    lax.fori_loop(0, own_count, select, 0)

    own_near.wait_send()

    @pl.when(inner)
    def _():
        own_far.wait_send()
        near_to_far.wait_send()
        far_to_near.wait_send()
        rest_to_near.wait_send()

    for k in range(4):
        plane_copy(k, FROM_X, e, ex).wait_send()
        plane_copy(k, FROM_Y, e, ey).wait_send()
        plane_copy(k, CORE_OWN, e, ec).wait_send()
        plane_copy(k, DIAG_A, ex, ey).wait_send()
        plane_copy(k, CORE_X, ex, ec).wait_send()
        plane_copy(k, DIAG_B, ey, ex).wait_send()
        plane_copy(k, CORE_Y, ey, ec).wait_send()
        plane_copy(k, CORE_D, ed, ec).wait_send()


def gathered_shards(record, requested, partners, codes, counts):
    stations, comps, _, window_len = record.shape
    owners, capacity = requested.shape[1:]
    traces = stations * comps
    windows = lax.axis_size("tm")
    own_count = traces // windows
    blocks_in, lag_blocks = window_len // BLOCK, LAGS // BLOCK
    pool = owners * capacity * comps
    depth = (blocks_in + lag_blocks - 3) * BLOCK
    slots = partners.shape[2]
    cc_shape = jax.ShapeDtypeStruct((own_count, lag_blocks * pool, BLOCK), jnp.float32)
    dims = (traces, blocks_in, owners, capacity, comps, own_count, lag_blocks)
    vmem = pl.BlockSpec(memory_space=pltpu.VMEM)
    return pl.pallas_call(
        functools.partial(exchange_kernel, dims, 1.0 / math.sqrt(window_len * windows)),
        out_shape=jax.ShapeDtypeStruct((1, own_count * slots, LAGS), jnp.float32),
        in_specs=[pl.BlockSpec(memory_space=pltpu.HBM)] * 5,
        out_specs=vmem,
        scratch_shapes=[pltpu.VMEM((owners, traces, blocks_in, BLOCK), jnp.bfloat16)] * 4
        + [
            pltpu.SMEM((owners, capacity, owners), jnp.int32),
            pltpu.VMEM((comps, stations, window_len), jnp.bfloat16),
            pltpu.VMEM((2, traces * blocks_in, HALF), jnp.float32),
            pltpu.VMEM((2, pool * blocks_in, HALF), jnp.float32),
            pltpu.VMEM((own_count, blocks_in, BLOCK), jnp.float32),
            pltpu.VMEM((blocks_in, pool, BLOCK), jnp.bfloat16),
            pltpu.VMEM((4 * own_count, HALF, depth + HALF), jnp.bfloat16),
            pltpu.SemaphoreType.DMA((4, 8)),
            pltpu.SemaphoreType.DMA((4, 8)),
            pltpu.SemaphoreType.DMA((5,)),
            pltpu.SemaphoreType.DMA((3,)),
            pltpu.SemaphoreType.DMA((5,)),
            pltpu.VMEM(cc_shape.shape, jnp.float32),
            pltpu.SMEM(counts.shape, jnp.int32),
            pltpu.VMEM((traces, 1, slots), jnp.int32),
            pltpu.VMEM((traces, 1, slots), jnp.int32),
        ],
        compiler_params=pltpu.CompilerParams(
            collective_id=0, has_side_effects=True, vmem_limit_bytes=60 * 1024 * 1024
        ),
    )(
        requested.transpose(0, 2, 1),
        record.transpose(2, 1, 0, 3)[0],
        counts,
        partners.transpose(1, 0, 2),
        codes.transpose(1, 0, 2),
    )


def solution(mesh):
    def body(record, requested, partners, codes, counts):
        planes = lax.axis_size("tm") == 4 and lax.axis_size("pairs") == 8
        stations, comps, window_count, window_len = record.shape
        fits = (
            window_count == 1
            and stations == 4
            and window_len % (8 * BLOCK) == 0
            and LAGS == 4 * BLOCK
        )
        form = gathered_shards if planes and fits else shards
        return form(record, requested, partners, codes, counts)

    return jax.shard_map(
        body,
        mesh=mesh,
        in_specs=(
            P("pairs", None, "tm", None),
            P(),
            P("pairs", None, None),
            P("pairs", None, None),
            P("pairs", None),
        ),
        out_specs=P("pairs", "tm", None),
        check_vma=False,
    )
```

```python
import functools
import math

import jax
import jax.numpy as jnp
from jax import lax
from jax.experimental import pallas as pl
from jax.experimental.pallas import tpu as pltpu
from jax.sharding import PartitionSpec as P

LAGS = 1024


def normalize(traces):
    values = traces.astype(jnp.float32)
    values = values - jnp.mean(values, axis=-1, keepdims=True)
    power_mean = jnp.mean(values * values, axis=-1, keepdims=True)
    return (values * lax.rsqrt(power_mean + 1e-06)).astype(jnp.bfloat16)


def correlate(own_trace, partner_rows, lag_count, block_len):
    window_len = own_trace.shape[0]
    half_lag = lag_count // 2
    padded = jnp.pad(own_trace, (half_lag, half_lag + block_len))
    length = padded.shape[0]
    spread = jnp.broadcast_to(padded, (block_len, length)).reshape(-1)
    spread = jnp.pad(spread, (0, block_len))
    skewed = spread.reshape(block_len, length + 1)[:, : window_len + lag_count]
    hankel = skewed.reshape(block_len, (window_len + lag_count) // block_len, block_len)
    blocks_in = window_len // block_len
    pieces = partner_rows.reshape(partner_rows.shape[0], blocks_in, block_len)
    outputs = []
    for offset in range(lag_count // block_len):
        window_view = hankel[:, offset : offset + blocks_in, :]
        outputs.append(
            jnp.einsum("pmi,imr->pr", pieces, window_view, preferred_element_type=jnp.float32)
        )
    return jnp.concatenate(outputs, axis=1)


def shards(record, requested, partners, codes, counts):
    whitened = normalize(record)
    local_stations, comp_count, window_count, window_len = whitened.shape
    owners = lax.axis_size("pairs")
    capacity = requested.shape[2]
    per_trace = partners.shape[2]
    trace_count = local_stations * comp_count
    block_len = math.gcd(math.gcd(128, window_len), LAGS)
    own_index = lax.axis_index("pairs")
    slot_ids = partners[0]
    comp_ids = codes[0]
    everyone = lax.all_gather(whitened, "pairs", axis=0, tiled=True)
    trace_pool = everyone.reshape(owners * local_stations * comp_count, window_count, window_len)
    asked_table = lax.dynamic_index_in_dim(requested, own_index, axis=0, keepdims=False)
    station_of = (
        asked_table + jnp.arange(owners, dtype=jnp.int32)[:, None] * local_stations
    ).reshape(-1)
    matches = slot_ids[:, :, None] == jnp.arange(owners * capacity, dtype=jnp.int32)[None, None, :]
    stations = jnp.sum(jnp.where(matches, station_of[None, None, :], 0), axis=-1)
    row_ids = stations * comp_count + comp_ids
    picked = jnp.take(trace_pool, row_ids.reshape(-1), axis=0)
    live_rows = jnp.arange(per_trace, dtype=jnp.int32)[None, :] < counts[0][:, None]
    picked = jnp.where(live_rows.reshape(-1)[:, None, None], picked, jnp.zeros((), jnp.bfloat16))
    picked = picked.reshape(trace_count, per_trace, window_count, window_len)
    picked = jnp.moveaxis(picked, 2, 1).reshape(trace_count * window_count, per_trace, window_len)
    own_rows = whitened.reshape(trace_count * window_count, window_len)

    def one_trace(operands):
        own_row, partner_rows = operands
        return correlate(own_row, partner_rows, LAGS, block_len)

    lagged = lax.map(one_trace, (own_rows, picked))
    lagged = lagged.reshape(trace_count, window_count, per_trace, LAGS)
    total_windows = window_count * lax.axis_size("tm")
    window_term = jnp.sum(lagged, axis=1) * (1.0 / math.sqrt(window_len * total_windows))
    window_term = window_term.reshape(1, trace_count * per_trace, LAGS)
    return lax.psum_scatter(window_term, "tm", scatter_dimension=1, tiled=True)


MESH = pl.DeviceIdType.MESH
HALF = 128
BLOCK = 2 * HALF
FROM_X, FROM_Y, DIAG_A, DIAG_B, CORE_OWN, CORE_X, CORE_Y, CORE_D = range(8)


def exchange_kernel(
    dims, asked_ref, record_ref, cc_ref, *scratch
):
    traces, blocks_in, owners, capacity, comps, own_count, lag_blocks = dims
    blks = scratch[:4]
    (rows32, pool32, own32, pool16, hankel) = scratch[4:9]
    (send, recv, zsend, zrecv) = scratch[9:]
    pool = owners * capacity * comps
    first_s, last_s = 1, blocks_in + lag_blocks - 3
    t = lax.axis_index("tm")
    e = lax.axis_index("pairs")
    core, x, y = lax.rem(e, 2), lax.rem(e // 2, 2), e // 4
    ex, ey, ec = e + 2 - 4 * x, e + 4 - 8 * y, e + 1 - 2 * core
    ed = ex + 4 - 8 * y
    cx, cy, cd = ex + 1 - 2 * core, ey + 1 - 2 * core, ed + 1 - 2 * core

    near, far = t + 1 - 2 * lax.rem(t, 2), 3 - t
    inner = (t == 1) | (t == 2)

    barrier = pltpu.get_barrier_semaphore()
    for peer in ((t, ex), (t, ey), (t, ec), (near, e), (far, e)):
        pl.semaphore_signal(barrier, inc=1, device_id=peer, device_id_type=MESH)

    row_index = lax.broadcasted_iota(jnp.int32, (HALF, HALF), 0)
    lane_index = lax.broadcasted_iota(jnp.int32, (HALF, HALF), 1)
    mirror = jnp.where(row_index + lane_index == HALF - 1, 1.0, 0.0).astype(jnp.bfloat16)

    def flip_halves(tile):
        return jnp.dot(tile, mirror, preferred_element_type=jnp.float32)

    stations = traces // comps

    def whiten(comp, carry):
        values = record_ref[comp].astype(jnp.float32)
        values = values - jnp.mean(values, axis=-1, keepdims=True)
        power_mean = jnp.mean(values * values, axis=-1, keepdims=True)
        values = values * lax.rsqrt(power_mean + 1e-06)
        for m in range(blocks_in):
            rows = pl.ds(comp * blocks_in + m, stations, stride=comps * blocks_in)
            for h in (0, 1):
                lane = m * BLOCK + h * HALF
                rows32[h, rows, :] = values[:, lane : lane + HALF]
        return carry

    lax.fori_loop(0, comps, whiten, 0)
    for h in (0, 1):
        blks[0][e, :, :, h * HALF : (h + 1) * HALF] = (
            flip_halves(rows32[h].astype(jnp.bfloat16))
            .astype(jnp.bfloat16)
            .reshape(traces, blocks_in, HALF)
        )
    pl.semaphore_wait(barrier, 5)

    def plane_copy(k, kind, origin, target):
        blk = blks[k]
        if kind == DIAG_A:
            ref = blk.at[origin, pl.ds(0, traces // 2)]
        elif kind == DIAG_B:
            ref = blk.at[origin, pl.ds(traces // 2, traces // 2)]
        else:
            ref = blk.at[origin]
        return pltpu.make_async_remote_copy(
            src_ref=ref, dst_ref=ref,
            send_sem=send.at[k, kind], recv_sem=recv.at[k, kind],
            device_id=(t, target), device_id_type=MESH,
        )

    def z_copy(index, source, slot, target):
        return pltpu.make_async_remote_copy(
            src_ref=blks[source].at[e], dst_ref=blks[slot].at[e],
            send_sem=zsend.at[index], recv_sem=zrecv.at[slot - 1],
            device_id=(target, e), device_id_type=MESH,
        )

    own_near = z_copy(0, 0, 1, near)
    own_far = z_copy(1, 0, 2, far)
    near_to_far = z_copy(2, 1, 3, far)
    far_to_near = z_copy(3, 2, 2, near)
    rest_to_near = z_copy(4, 3, 3, near)

    def wait_window(k):
        z_copy(0, 0, k, near).wait_recv()

    def send_own(k):
        plane_copy(k, FROM_X, e, ex).start()
        plane_copy(k, FROM_Y, e, ey).start()
        plane_copy(k, CORE_OWN, e, ec).start()

    def forward_xy(k):
        plane_copy(k, FROM_X, ex, ex).wait_recv()
        plane_copy(k, DIAG_A, ex, ey).start()
        plane_copy(k, CORE_X, ex, ec).start()
        plane_copy(k, FROM_Y, ey, ey).wait_recv()
        plane_copy(k, DIAG_B, ey, ex).start()
        plane_copy(k, CORE_Y, ey, ec).start()

    def forward_diag(k):
        plane_copy(k, DIAG_A, ed, ey).wait_recv()
        plane_copy(k, DIAG_B, ed, ex).wait_recv()
        plane_copy(k, CORE_D, ed, ec).start()

    def wait_core(k):
        plane_copy(k, CORE_OWN, ec, ec).wait_recv()
        plane_copy(k, CORE_X, cx, ec).wait_recv()
        plane_copy(k, CORE_Y, cy, ec).wait_recv()
        plane_copy(k, CORE_D, cd, ec).wait_recv()

    below = lane_index <= row_index
    nothing = jnp.zeros((HALF, HALF), jnp.bfloat16)
    first_chunk = 2 * first_s

    last_chunk = 2 * last_s + 2

    def unmirror(k):
        for j in range(own_count):
            for h in (0, 1):
                lanes = slice(h * HALF, (h + 1) * HALF)
                own32[j, :, lanes] = flip_halves(blks[k][e, own_count * t + j, :, lanes])

    def build(n):
        def one(j, carry):
            index = own_count * n + j

            def eight_blocks(g, before):
                rows = own32[j, pl.ds(pl.multiple_of(8 * g, 8), 8), :]
                for b in range(8):
                    m = 8 * g + b
                    for half in (0, 1):
                        row = rows[b : b + 1, half * HALF : (half + 1) * HALF]
                        skewed = pltpu.roll(
                            jnp.broadcast_to(row, (16, HALF)), 1, 1, stride=1, stride_axis=0
                        ).astype(jnp.bfloat16)
                        now = jnp.concatenate(
                            [skewed] + [pltpu.roll(skewed, 16 * a, 1) for a in range(1, HALF // 16)],
                            axis=0,
                        )
                        lane = (2 * m + half + lag_blocks - 1 - first_chunk) * HALF
                        hankel[index, :, pl.ds(pl.multiple_of(lane, HALF), HALF)] = jnp.where(
                            below, before, now
                        )
                        before = now
                return before

            before = lax.fori_loop(0, blocks_in // 8, eight_blocks, nothing)
            lane = (2 * blocks_in + lag_blocks - 1 - first_chunk) * HALF
            hankel[index, :, lane : lane + HALF] = jnp.where(below, before, nothing)
            hankel[index, :, :HALF] = nothing
            lane = (last_chunk - first_chunk) * HALF
            hankel[index, :, lane : lane + HALF] = nothing
            return carry

        lax.fori_loop(0, own_count, one, 0)

    def pick(k):
        blk = blks[k]

        def one(slot, carry):
            d, i = slot // capacity, lax.rem(slot, capacity)
            station = asked_ref[e, i, d]
            rows = (
                blk[d, pl.ds(station * comps, comps)]
                .astype(jnp.float32)
                .reshape(comps * blocks_in, BLOCK)
            )
            start = pl.multiple_of(slot * (comps * blocks_in), comps * blocks_in)
            for h in (0, 1):
                pool32[h, pl.ds(start, comps * blocks_in), :] = rows[:, h * HALF : (h + 1) * HALF]
            return carry

        lax.fori_loop(0, owners * capacity, one, 0)

    def correlate(n):
        for m in range(blocks_in):
            for h in (0, 1):
                part = pool32[h, pl.ds(m, pool, stride=blocks_in), :].astype(jnp.bfloat16)
                pool16[m, :, h * HALF : (h + 1) * HALF] = part

        pl.when(n == 2)(functools.partial(forward_diag, 3))
        empty = jnp.zeros((pool, BLOCK), jnp.bfloat16)
        left = jnp.concatenate(
            [
                jnp.concatenate(
                    [
                        pool16[s - q] if 0 <= s - q < blocks_in else empty
                        for s in range(first_s, last_s + 1)
                    ],
                    axis=1,
                )
                for q in reversed(range(lag_blocks))
            ],
            axis=0,
        )
        right = jnp.concatenate(
            [
                jnp.concatenate(
                    [hankel[own_count * n + j, :, lane : lane + BLOCK] for j in range(own_count)], axis=1
                )
                for s in range(first_s, last_s + 1)
                for lane in ((2 * s - first_chunk) * HALF, (2 * s + 1 - first_chunk) * HALF)
            ],
            axis=0,
        )
        term = jnp.dot(left, right, preferred_element_type=jnp.float32)

        @pl.when(n == 0)
        def _():
            for j in range(own_count):
                cc_ref[j] = term[:, j * BLOCK : (j + 1) * BLOCK]

        @pl.when(n > 0)
        def _():
            for j in range(own_count):
                cc_ref[j] += term[:, j * BLOCK : (j + 1) * BLOCK]

    own_near.start()

    @pl.when(inner)
    def _():
        own_far.start()

    send_own(0)
    def before_build(n):
        if n == 1:
            wait_window(1)

            @pl.when(inner)
            def _():
                near_to_far.start()
                wait_window(2)
                far_to_near.start()

            send_own(1)
            forward_xy(0)
        if n == 2:
            forward_diag(0)

            @pl.when(jnp.logical_not(inner))
            def _():
                wait_window(2)

            @pl.when(inner)
            def _():
                wait_window(3)
                rest_to_near.start()

            send_own(2)
            forward_xy(1)
        if n == 3:
            forward_diag(1)

            @pl.when(jnp.logical_not(inner))
            def _():
                wait_window(3)

            send_own(3)
            forward_xy(2)
        if n == 4:
            forward_diag(2)
            forward_xy(3)
        if n < 4:
            unmirror(n)

    def before_correlate(n):
        wait_core(n)
        pick(n)

    def step(n, carry):
        for k in range(5):
            pl.when(n == k)(functools.partial(before_build, k))
        pl.when(n < 4)(functools.partial(build, n))
        for k in range(4):
            pl.when(n == k + 2)(functools.partial(before_correlate, k))
        pl.when(n >= 2)(functools.partial(correlate, n - 2))
        return carry

    lax.fori_loop(0, 6, step, 0)

    own_near.wait_send()

    @pl.when(inner)
    def _():
        own_far.wait_send()
        near_to_far.wait_send()
        far_to_near.wait_send()
        rest_to_near.wait_send()

    for k in range(4):
        plane_copy(k, FROM_X, e, ex).wait_send()
        plane_copy(k, FROM_Y, e, ey).wait_send()
        plane_copy(k, CORE_OWN, e, ec).wait_send()
        plane_copy(k, DIAG_A, ex, ey).wait_send()
        plane_copy(k, CORE_X, ex, ec).wait_send()
        plane_copy(k, DIAG_B, ey, ex).wait_send()
        plane_copy(k, CORE_Y, ey, ec).wait_send()
        plane_copy(k, CORE_D, ed, ec).wait_send()


def select_kernel(scale, own_count, comps, lag_blocks, counts_ref, partners_ref, codes_ref, cc_ref, out_ref):
    pool = cc_ref.shape[1] // lag_blocks
    slots = partners_ref.shape[2]
    pool_row = lax.broadcasted_iota(jnp.int32, (pool, slots), 0)
    slot_lane = lax.broadcasted_iota(jnp.int32, (pool, slots), 1)
    dims = (((0,), (0,)), ((), ()))

    def one(j, carry):
        trace = own_count * lax.axis_index("tm") + j
        wanted = partners_ref[trace] * comps + codes_ref[trace]
        hit = (wanted == pool_row) & (slot_lane < counts_ref[0, trace])
        chosen = jnp.where(hit, 1.0, 0.0).astype(jnp.bfloat16)
        rows = pl.ds(pl.multiple_of(j * slots, 8), slots)
        for q in range(lag_blocks):
            part = cc_ref[j, q * pool : (q + 1) * pool, :]
            high = part.astype(jnp.bfloat16)
            low = (part - high.astype(jnp.float32)).astype(jnp.bfloat16)
            total = lax.dot_general(chosen, low, dims, preferred_element_type=jnp.float32)
            total += lax.dot_general(chosen, high, dims, preferred_element_type=jnp.float32)
            lag = (lag_blocks - 1 - q) * BLOCK
            out_ref[0, rows, lag : lag + BLOCK] = total * scale
        return carry

    lax.fori_loop(0, own_count, one, 0)


def gathered_shards(record, requested, partners, codes, counts):
    stations, comps, _, window_len = record.shape
    owners, capacity = requested.shape[1:]
    traces = stations * comps
    windows = lax.axis_size("tm")
    own_count = traces // windows
    blocks_in, lag_blocks = window_len // BLOCK, LAGS // BLOCK
    pool = owners * capacity * comps
    depth = (blocks_in + lag_blocks - 3) * BLOCK
    slots = partners.shape[2]
    cc_shape = jax.ShapeDtypeStruct((own_count, lag_blocks * pool, BLOCK), jnp.float32)
    dims = (traces, blocks_in, owners, capacity, comps, own_count, lag_blocks)
    vmem = pl.BlockSpec(memory_space=pltpu.VMEM)
    smem = pl.BlockSpec(memory_space=pltpu.SMEM)
    cc = pl.pallas_call(
        functools.partial(exchange_kernel, dims),
        out_shape=cc_shape,
        in_specs=[smem, vmem],
        out_specs=vmem,
        scratch_shapes=[pltpu.VMEM((owners, traces, blocks_in, BLOCK), jnp.bfloat16)] * 4
        + [
            pltpu.VMEM((2, traces * blocks_in, HALF), jnp.float32),
            pltpu.VMEM((2, pool * blocks_in, HALF), jnp.float32),
            pltpu.VMEM((own_count, blocks_in, BLOCK), jnp.float32),
            pltpu.VMEM((blocks_in, pool, BLOCK), jnp.bfloat16),
            pltpu.VMEM((4 * own_count, HALF, depth + HALF), jnp.bfloat16),
            pltpu.SemaphoreType.DMA((4, 8)),
            pltpu.SemaphoreType.DMA((4, 8)),
            pltpu.SemaphoreType.DMA((5,)),
            pltpu.SemaphoreType.DMA((3,)),
        ],
        compiler_params=pltpu.CompilerParams(
            collective_id=0, has_side_effects=True, vmem_limit_bytes=40 * 1024 * 1024
        ),
    )(requested.transpose(0, 2, 1), record.transpose(2, 1, 0, 3)[0])
    return pl.pallas_call(
        functools.partial(
            select_kernel, 1.0 / math.sqrt(window_len * windows), own_count, comps, lag_blocks
        ),
        out_shape=jax.ShapeDtypeStruct((1, own_count * slots, LAGS), jnp.float32),
        in_specs=[smem, vmem, vmem, vmem],
        out_specs=vmem,
        compiler_params=pltpu.CompilerParams(vmem_limit_bytes=16 * 1024 * 1024),
    )(counts, partners.transpose(1, 0, 2), codes.transpose(1, 0, 2), cc)


def solution(mesh):
    def body(record, requested, partners, codes, counts):
        planes = lax.axis_size("tm") == 4 and lax.axis_size("pairs") == 8
        stations, comps, window_count, window_len = record.shape
        fits = (
            window_count == 1
            and stations == 4
            and window_len % (8 * BLOCK) == 0
            and LAGS == 4 * BLOCK
        )
        form = gathered_shards if planes and fits else shards
        return form(record, requested, partners, codes, counts)

    return jax.shard_map(
        body,
        mesh=mesh,
        in_specs=(
            P("pairs", None, "tm", None),
            P(),
            P("pairs", None, None),
            P("pairs", None, None),
            P("pairs", None),
        ),
        out_specs=P("pairs", "tm", None),
        check_vma=False,
    )
```
